32 devices in a mesh: seq: 4 (over y, x), tp: 8 (over z, core).
Axes of the slice: x: 2, y: 2, z: 4, core: 2. Of those that a mesh axis runs over, the one named last changes fastest.
Arguments:
- projected: bfloat16 [3, 4096, 8192], P(None, 'seq', 'tp'), may hold values from -6 to 6
- short_filter: float32 [3, 3, 8192], P(None, None, 'tp'), may hold values from -2.5 to 2.5
- residue: float32 [512, 16], P('tp'), may hold values from -1.5 to 1.5
- rate: float32 [512, 16], P('tp'), may hold values from 0 to 1, as said below
- out_weight: bfloat16 [8192, 8192], P('tp'), may hold values from -0.0625 to 0.0625
Outputs:
- output: bfloat16 [4096, 8192], P(('seq', 'tp'))
The draws below stay inside these ranges and needn't reach their ends.
Inputs may be any that keep to these rules, and one draw needn't show every extreme that they name: Every rate is positive.
All inputs are finite; a program needn't handle non-finite values.
Results may differ from the reference program's by a relative error of at most 0.02.
Values may be sent and summed in bfloat16 or wider, within the bound.
A program may use at most 128 MiB of HBM per device.

```python
import jax
import jax.numpy as jnp
from jax import lax

D = 8192
GROUP = 16
MODES = 16
SEQ_LEN = 4096
GROUPS = 512


def draw_rate(key, part):
    lowest = jnp.log(0.02 / SEQ_LEN)
    highest = jnp.log(1.0 / 30.0)
    spread = jax.random.uniform(key, (GROUPS, MODES), jnp.float32)
    logged = lowest + spread * (highest - lowest)
    return jnp.exp(logged).astype(jnp.float32)


def levels(own_key, shape, shards, least, high):
    def one(dim, blocks):
        heights = jax.random.uniform(jax.random.fold_in(jax.random.fold_in(own_key, 6), dim), (blocks,), jnp.float32, least / len(shards), high / len(shards))
        return jnp.repeat(jnp.exp(heights), shape[dim] // blocks).reshape((-1,) + (1,) * (len(shape) - dim - 1))

    loudness = one(*shards[0])
    for cut in shards[1:]:
        loudness = loudness * one(*cut)
    return loudness


def centred(rng, shape, deviation, bound, shards=(), kind=jnp.bfloat16):
    entries = jax.random.normal(rng, shape, jnp.float32) * deviation
    if len(shards) > 0:
        entries = levels(rng, shape, shards, -0.22, 0.18) * entries
    return jnp.clip(entries, min=-bound, max=bound).astype(kind)


def setup_inputs(seed: int = 0) -> dict:
    seeds = jax.random.split(jax.random.key(seed), 6)
    projected = centred(seeds[0], (3, SEQ_LEN, D), 1.0, 6.0, ((1, 4), (2, 8)))
    short_filter = centred(seeds[1], (3, 3, D), 0.5, 2.5, ((2, 8),), jnp.float32)
    residue = centred(seeds[2], (GROUPS, MODES), 0.25, 1.5, ((0, 8),), jnp.float32)
    rate = draw_rate(jax.random.fold_in(seeds[5], 71), 0)
    out_weight = centred(seeds[4], (D, D), D ** -0.5, 0.0625, ((0, 8),))
    return dict(projected=projected, short_filter=short_filter, residue=residue, rate=rate, out_weight=out_weight)


def filter_tables(rate, residue, block_len):
    mode_weight = residue * jnp.sqrt(-jnp.expm1(-2.0 * rate))
    offsets = lax.iota(jnp.int32, block_len)
    lag_float = offsets.astype(jnp.float32)
    powers = jnp.exp(-rate[None, :, :] * lag_float[:, None, None])
    kernel = jnp.einsum('tgn,gn->gt', powers, mode_weight, precision=lax.Precision.HIGHEST)
    lagged = offsets[:, None] - offsets[None, :]
    clipped = jnp.clip(lagged, 0, block_len - 1).astype(jnp.int32)
    toeplitz = jnp.where(lagged[None] >= 0, kernel[:, clipped], jnp.float32(0.0))
    decay_into = jnp.exp(-rate[None, :, :] * (lag_float[:, None, None] + 1.0)) * mode_weight[None]
    decay_out = jnp.exp(-rate[None, :, :] * (block_len - 1.0 - lag_float)[:, None, None])
    block_power = jnp.exp(-rate * block_len)
    return (toeplitz, decay_into, decay_out, block_power)

def causal_conv(signal, tables, state_start):
    toeplitz, decay_into, decay_out, block_power = tables
    block_len = toeplitz.shape[1]
    row_count, group_count, group_width = signal.shape
    segments = signal.reshape(row_count // block_len, block_len, group_count, group_width)

    def advance(state_in, segment):
        within = jnp.einsum('gts,sgi->tgi', toeplitz, segment, precision=lax.Precision.HIGHEST)
        carried = jnp.einsum('tgn,gni->tgi', decay_into, state_in, precision=lax.Precision.HIGHEST)
        state_next = block_power[:, :, None] * state_in + jnp.einsum('tgn,tgi->gni', decay_out, segment, precision=lax.Precision.HIGHEST)
        return (state_next, within + carried)
    state_end, outputs = lax.scan(advance, state_start, segments)
    return (outputs.reshape(row_count, group_count, group_width), state_end)

def featurize(projected, short_filter):
    values = projected.astype(jnp.float32)
    length = values.shape[1]
    padded = jnp.concatenate([jnp.zeros((3, 2, values.shape[2]), jnp.float32), values], axis=1)
    return short_filter[:, 0, None, :] * padded[:, 2:] + short_filter[:, 1, None, :] * padded[:, 1:length + 1] + short_filter[:, 2, None, :] * padded[:, 0:length]

def reference(projected, short_filter, residue, rate, out_weight):
    featured = featurize(projected, short_filter)
    signal = featured[1] * featured[2]
    length = signal.shape[0]
    tables = filter_tables(rate, residue, min(256, length))
    grouped = signal.reshape(length, GROUPS, GROUP)
    conv = causal_conv(grouped, tables, jnp.zeros((GROUPS, MODES, GROUP), jnp.float32))[0]
    mixed = (featured[0] * conv.reshape(length, D)).astype(jnp.bfloat16)
    return jnp.dot(mixed, out_weight, preferred_element_type=jnp.float32).astype(jnp.bfloat16)
```

```python
import jax
import jax.numpy as jnp
from jax import lax
from jax.experimental import pallas as pl
from jax.experimental.pallas import tpu as pltpu
from jax.sharding import PartitionSpec as P

GROUP = 16
MODES = 16
MESH = pl.DeviceIdType.MESH


def passed_along(value, axis, steps):
    count = lax.axis_size(axis)
    leading, last = (max(0, -steps), min(count, count - steps))
    return lax.ppermute(value, axis, [(source, source + steps) for source in range(leading, last)])


def toeplitz_from(kernel, block_len):
    group_count = kernel.shape[0]
    padded = jnp.concatenate(
        [
            jnp.zeros((group_count, block_len - 1), jnp.float32),
            kernel,
            jnp.zeros((group_count, 1), jnp.float32),
        ],
        axis=1,
    )
    tiled = jnp.tile(padded, (1, block_len))
    width = 2 * block_len - 1
    trimmed = tiled[:, : block_len * width].reshape(group_count, block_len, width)
    hankel = trimmed[:, :, block_len - 1 : width]
    return jnp.swapaxes(hankel, 1, 2)


def filter_tables(rate, residue, block_len):
    mode_weight = residue * jnp.sqrt(-jnp.expm1(-2.0 * rate))
    offsets = lax.iota(jnp.int32, block_len)
    lag_float = offsets.astype(jnp.float32)
    powers = jnp.exp(-rate[None, :, :] * lag_float[:, None, None])
    kernel = jnp.einsum("tgn,gn->gt", powers, mode_weight, precision=lax.Precision.HIGHEST)
    toeplitz = toeplitz_from(kernel, block_len)
    decay_into = jnp.exp(-rate[None, :, :] * (lag_float[:, None, None] + 1.0)) * mode_weight[None]
    decay_out = jnp.exp(-rate[None, :, :] * (block_len - 1.0 - lag_float)[:, None, None])
    block_power = jnp.exp(-rate * block_len)
    return (toeplitz, decay_into, decay_out, block_power)


def causal_conv(signal, tables, state_start):
    toeplitz, decay_into, decay_out, block_power = tables
    block_len = toeplitz.shape[1]
    row_count, group_count, group_width = signal.shape
    segments = signal.reshape(row_count // block_len, block_len, group_count, group_width)

    def advance(state_in, segment):
        within = jnp.einsum("gts,sgi->tgi", toeplitz, segment, precision=lax.Precision.HIGHEST)
        carried = jnp.einsum("tgn,gni->tgi", decay_into, state_in, precision=lax.Precision.HIGHEST)
        state_next = block_power[:, :, None] * state_in + jnp.einsum(
            "tgn,tgi->gni", decay_out, segment, precision=lax.Precision.HIGHEST
        )
        return (state_next, within + carried)

    state_end, outputs = lax.scan(advance, state_start, segments)
    return (outputs.reshape(row_count, group_count, group_width), state_end)


def tile_count(chips):
    return max(1, 32 // chips)


def project_and_scatter(mixed, out_weight):
    tokens, depth = mixed.shape
    width = out_weight.shape[1]
    ranks = lax.axis_size("tp")
    chips = ranks // 2
    rows = tokens // ranks
    tiles = tile_count(chips)
    cols = width // tiles
    piece = min(256, cols)
    lag = 2
    slots = (chips - 1) * tiles

    def kernel(mixed_ref, w_ref, out_ref, w_buf, acc, stage, sib, inc,
               w_sem, sib_send, sib_recv, fwd_send, in_recv, out_sem):
        rank = lax.axis_index("tp")
        z = lax.div(rank, 2)
        core = lax.rem(rank, 2)
        partner = z * 2 + (1 - core)
        above = rank + 2
        below = rank - 2

        def w_copy(i):
            return pltpu.make_async_copy(
                w_ref.at[:, pl.ds(pl.multiple_of(i * cols, cols), cols)], w_buf.at[i], w_sem.at[i]
            )

        @pl.loop(0, tiles)
        def _(i):
            w_copy(i).start()

        barrier = pltpu.get_barrier_semaphore()
        pl.semaphore_signal(barrier, inc=1, device_id={"tp": partner}, device_id_type=MESH)

        @pl.when(z < chips - 1)
        def _():
            pl.semaphore_signal(barrier, inc=1, device_id={"tp": above}, device_id_type=MESH)

        @pl.when(z > 0)
        def _():
            pl.semaphore_signal(barrier, inc=1, device_id={"tp": below}, device_id_type=MESH)

        middle = jnp.logical_and(z > 0, z < chips - 1)

        @pl.when(middle)
        def _():
            pl.semaphore_wait(barrier, 3)

        @pl.when(jnp.logical_not(middle))
        def _():
            pl.semaphore_wait(barrier, 2)

        def sib_copy(dest, i):
            return pltpu.make_async_remote_copy(
                src_ref=stage.at[dest, i], dst_ref=sib.at[dest, i],
                send_sem=sib_send.at[dest, i], recv_sem=sib_recv.at[dest, i],
                device_id={"tp": partner}, device_id_type=MESH,
            )

        def fwd_copy(dest, i, landing, target):
            return pltpu.make_async_remote_copy(
                src_ref=acc.at[dest, i], dst_ref=inc.at[landing, i],
                send_sem=fwd_send.at[dest, i], recv_sem=in_recv.at[landing, i],
                device_id={"tp": target}, device_id_type=MESH,
            )

        def compute(dest, i):
            base = dest * (2 * rows)
            own = mixed_ref[pl.ds(pl.multiple_of(base + core * rows, rows), rows), :]
            other = mixed_ref[pl.ds(pl.multiple_of(base + (1 - core) * rows, rows), rows), :]
            left = jnp.concatenate([own, other], axis=0)

            @pl.loop(0, cols // piece)
            def _(p):
                at = pl.ds(pl.multiple_of(p * piece, piece), piece)
                product = jnp.dot(left, w_buf[i, :, at], preferred_element_type=jnp.float32)
                acc[dest, i, :, at] = product[:rows].astype(jnp.bfloat16)
                stage[dest, i, :, at] = product[rows:].astype(jnp.bfloat16)

            sib_copy(dest, i).start()

        def add_in(dest, i, landing):
            @pl.loop(0, cols // piece)
            def _(p):
                at = pl.ds(pl.multiple_of(p * piece, piece), piece)
                total = acc[dest, i, :, at].astype(jnp.float32) + inc[landing, i, :, at].astype(jnp.float32)
                acc[dest, i, :, at] = (total + sib[dest, i, :, at].astype(jnp.float32)).astype(jnp.bfloat16)

        def add_sib(dest, i):
            @pl.loop(0, cols // piece)
            def _(p):
                at = pl.ds(pl.multiple_of(p * piece, piece), piece)
                total = acc[dest, i, :, at].astype(jnp.float32) + sib[dest, i, :, at].astype(jnp.float32)
                acc[dest, i, :, at] = total.astype(jnp.bfloat16)

        def up_place(k):
            return chips - 1 - lax.div(k, tiles), lax.rem(k, tiles)

        def down_place(k):
            return lax.div(k, tiles), lax.rem(k, tiles)

        up_count = (chips - 1 - z) * tiles
        down_count = z * tiles
        up_shift = z * lag
        down_shift = (chips - 1 - z) * lag
        up_first = jnp.where(z < chips - 1, up_shift, slots + lag * chips)
        down_first = jnp.where(z > 0, down_shift, slots + lag * chips)
        first = jnp.minimum(up_first, down_first)

        def forward(k, place, fed, landing_of, target):
            dest, i = place(k)

            @pl.when(k >= 2)
            def _():
                before, j = place(k - 2)
                fwd_copy(before, j, landing_of(before), target).wait_send()

            sib_copy(dest, i).wait_recv()

            @pl.when(fed)
            def _():
                fwd_copy(dest, i, dest, target).wait_recv()
                add_in(dest, i, dest)

            @pl.when(jnp.logical_not(fed))
            def _():
                add_sib(dest, i)

            fwd_copy(dest, i, landing_of(dest), target).start()

        def up_landing(dest):
            return dest

        def down_landing(dest):
            return jnp.where(dest == z - 1, chips, dest)

        @pl.loop(0, slots + 1)
        def _(it):
            w_at = it - first

            @pl.when(jnp.logical_and(w_at >= 0, w_at < tiles))
            def _():
                w_copy(w_at).wait()

            ku = it - up_shift

            @pl.when(jnp.logical_and(ku >= 0, ku < up_count))
            def _():
                dest, i = up_place(ku)
                compute(dest, i)

            kd = it - down_shift

            @pl.when(jnp.logical_and(kd >= 0, kd < down_count))
            def _():
                dest, i = down_place(kd)
                compute(dest, i)

            ks = it - first - tiles

            @pl.when(jnp.logical_and(ks >= 0, ks < tiles))
            def _():
                compute(z, ks)

            @pl.when(jnp.logical_and(ku >= 1, ku <= up_count))
            def _():
                forward(ku - 1, up_place, z > 0, up_landing, above)

            @pl.when(jnp.logical_and(kd >= 1, kd <= down_count))
            def _():
                forward(kd - 1, down_place, z < chips - 1, down_landing, below)

        def drain(count, place, landing_of, target):
            @pl.when(count >= 2)
            def _():
                for back in (2, 1):
                    dest, i = place(count - back)
                    fwd_copy(dest, i, landing_of(dest), target).wait_send()

            @pl.when(count == 1)
            def _():
                dest, i = place(count - 1)
                fwd_copy(dest, i, landing_of(dest), target).wait_send()

        def out_copy(i):
            return pltpu.make_async_copy(
                acc.at[z, i], out_ref.at[:, pl.ds(pl.multiple_of(i * cols, cols), cols)], out_sem.at[i]
            )

        @pl.loop(0, tiles)
        def _(i):
            sib_copy(z, i).wait_recv()

            @pl.when(z < chips - 1)
            def _():
                fwd_copy(z, i, chips, above).wait_recv()

            @pl.when(z > 0)
            def _():
                fwd_copy(z, i, z, below).wait_recv()

            @pl.when(z == 0)
            def _():
                add_in(z, i, chips)

            @pl.when(z == chips - 1)
            def _():
                add_in(z, i, z)

            @pl.when(middle)
            def _():
                @pl.loop(0, cols // piece)
                def _(p):
                    at = pl.ds(pl.multiple_of(p * piece, piece), piece)
                    total = acc[z, i, :, at].astype(jnp.float32) + sib[z, i, :, at].astype(jnp.float32)
                    total = total + inc[z, i, :, at].astype(jnp.float32)
                    total = total + inc[chips, i, :, at].astype(jnp.float32)
                    acc[z, i, :, at] = total.astype(jnp.bfloat16)

            out_copy(i).start()

        drain(up_count, up_place, up_landing, above)
        drain(down_count, down_place, down_landing, below)

        @pl.loop(0, tiles)
        def _(i):
            out_copy(i).wait()

            @pl.loop(0, chips)
            def _(dest):
                sib_copy(dest, i).wait_send()

    block = (chips, tiles, rows, cols)
    return pl.pallas_call(
        kernel,
        out_shape=jax.ShapeDtypeStruct((rows, width), jnp.bfloat16),
        in_specs=[pl.BlockSpec(memory_space=pltpu.VMEM), pl.BlockSpec(memory_space=pl.ANY)],
        out_specs=pl.BlockSpec(memory_space=pl.ANY),
        scratch_shapes=[
            pltpu.VMEM((tiles, depth, cols), jnp.bfloat16),
            pltpu.VMEM(block, jnp.bfloat16),
            pltpu.VMEM(block, jnp.bfloat16),
            pltpu.VMEM(block, jnp.bfloat16),
            pltpu.VMEM((chips + 1, tiles, rows, cols), jnp.bfloat16),
            pltpu.SemaphoreType.DMA((tiles,)),
            pltpu.SemaphoreType.DMA((chips, tiles)),
            pltpu.SemaphoreType.DMA((chips, tiles)),
            pltpu.SemaphoreType.DMA((chips, tiles)),
            pltpu.SemaphoreType.DMA((chips + 1, tiles)),
            pltpu.SemaphoreType.DMA((tiles,)),
        ],
        compiler_params=pltpu.CompilerParams(
            collective_id=0, has_side_effects=True, vmem_limit_bytes=60 * 1024 * 1024
        ),
        cost_estimate=pl.CostEstimate(
            flops=2 * tokens * depth * width, bytes_accessed=2 * depth * width, transcendentals=0
        ),
    )(mixed, out_weight)


def local(projected, short_filter, residue, rate, out_weight):
    row_count = projected.shape[1]
    channels = projected.shape[2]
    group_count = rate.shape[0]
    prior_rows = passed_along(projected[:, -2:, :], "seq", 1)
    extended = jnp.concatenate([prior_rows, projected], axis=1).astype(jnp.float32)
    featured = (
        short_filter[:, 0, None, :] * extended[:, 2:]
        + short_filter[:, 1, None, :] * extended[:, 1 : row_count + 1]
        + short_filter[:, 2, None, :] * extended[:, 0:row_count]
    )
    signal = (featured[1] * featured[2]).reshape(row_count, group_count, GROUP)
    tables = filter_tables(rate, residue, min(256, row_count))
    local_conv, local_end = causal_conv(
        signal, tables, jnp.zeros((group_count, MODES, GROUP), jnp.float32)
    )
    device_power = jnp.exp(-rate * row_count)[:, :, None]

    def relay_state(rounds, received):
        running = device_power * received + local_end
        return passed_along(running, "seq", 1)

    incoming = lax.fori_loop(0, lax.axis_size("seq") - 1, relay_state, jnp.zeros_like(local_end))
    lag_float = lax.iota(jnp.int32, row_count).astype(jnp.float32)
    mode_weight = residue * jnp.sqrt(-jnp.expm1(-2.0 * rate))
    reach = jnp.exp(-rate[None, :, :] * (lag_float[:, None, None] + 1.0)) * mode_weight[None]
    conv = local_conv + jnp.einsum("tgn,gni->tgi", reach, incoming, precision=lax.Precision.HIGHEST)
    mixed = (featured[0] * conv.reshape(row_count, channels)).astype(jnp.bfloat16)
    return project_and_scatter(mixed, out_weight)


def solution(mesh):
    placed = (
        P(None, "seq", "tp"),
        P(None, None, "tp"),
        P("tp", None),
        P("tp", None),
        P("tp", None),
    )
    return jax.shard_map(
        local, mesh=mesh, in_specs=placed, out_specs=P(("seq", "tp"), None), check_vma=False
    )
```

```python
import jax
import jax.numpy as jnp
from jax import lax
from jax.experimental import pallas as pl
from jax.experimental.pallas import tpu as pltpu
from jax.sharding import PartitionSpec as P

GROUP = 16
MODES = 16
MESH = pl.DeviceIdType.MESH
WINDOW = 32
LANES = 128


def split(value):
    high = value.astype(jnp.bfloat16)
    return high, (value - high.astype(jnp.float32)).astype(jnp.bfloat16)


def iota(shape, dim):
    return lax.broadcasted_iota(jnp.int32, shape, dim)


def mix(projected, short_filter, residue, rate):
    tokens, channels = projected.shape[1:]
    blocks = channels // LANES
    count = lax.axis_size("seq")
    chunk = min(256, tokens)
    chunks = tokens // chunk
    wide = chunks * LANES
    held = LANES // GROUP
    mode_weight = residue * jnp.sqrt(-jnp.expm1(-2.0 * rate))
    rows = jnp.stack([rate.reshape(blocks, LANES), mode_weight.reshape(blocks, LANES)], axis=1)
    down = jnp.broadcast_to(rate.reshape(channels, 1), (channels, LANES))

    def kernel(proj, taps, row_ref, down_ref, out, halo, ext, table, q_buf, x_buf, s_buf, y_buf,
               end, landed, state, halo_send, halo_recv, end_send, end_recv):
        me = lax.axis_index("seq")

        barrier = pltpu.get_barrier_semaphore()

        @pl.loop(1, count)
        def _(k):
            pl.semaphore_signal(
                barrier, inc=1, device_id={"seq": lax.rem(me + k, count)}, device_id_type=MESH
            )

        pl.semaphore_wait(barrier, count - 1)

        def halo_copy(target):
            return pltpu.make_async_remote_copy(
                src_ref=proj.at[:, pl.ds(tokens - 16, 16), :], dst_ref=halo,
                send_sem=halo_send, recv_sem=halo_recv,
                device_id={"seq": target}, device_id_type=MESH,
            )

        def end_copy(slot, k, target):
            return pltpu.make_async_remote_copy(
                src_ref=end, dst_ref=landed.at[slot],
                send_sem=end_send.at[k], recv_sem=end_recv.at[slot],
                device_id={"seq": target}, device_id_type=MESH,
            )

        @pl.when(me < count - 1)
        def _():
            halo_copy(me + 1).start()

        @pl.loop(0, blocks)
        def _(b):
            rate_row = row_ref[b, 0:1, :]
            weight_row = row_ref[b, 1:2, :]
            lag = iota((chunk, LANES), 0).astype(jnp.float32) - (WINDOW - 1.0)
            p_high, p_low = split(jnp.exp(-rate_row * lag) * weight_row)
            rate_down = down_ref[pl.ds(pl.multiple_of(b * LANES, LANES), LANES), :]
            rate_down = jnp.concatenate([rate_down] * (held * WINDOW // LANES), axis=1)
            shape = (LANES, held * WINDOW)
            place = lax.rem(iota(shape, 1), WINDOW).astype(jnp.float32) - (WINDOW - 1.0)
            same = lax.div(iota(shape, 0), MODES) == lax.div(iota(shape, 1), WINDOW)
            g_high, g_low = split(jnp.where(same, jnp.exp(rate_down * place), 0.0))
            filled = jnp.dot(
                jnp.concatenate([p_high, p_high, p_low], axis=1),
                jnp.concatenate([g_high, g_low, g_high], axis=0),
                preferred_element_type=jnp.float32,
            )
            shape = (chunk, held * WINDOW)
            causal = iota(shape, 0) >= lax.rem(iota(shape, 1), WINDOW)
            table[b] = jnp.where(causal, filled, 0.0).astype(jnp.bfloat16)

        @pl.when(me > 0)
        def _():
            halo_copy(me).wait_recv()

        @pl.when(me == 0)
        def _():
            halo[...] = jnp.zeros_like(halo)

        @pl.loop(0, blocks)
        def _(b):
            at = pl.ds(pl.multiple_of(b * LANES, LANES), LANES)
            for p in range(3):
                ext[p, 0:16, :] = halo[p, :, at].astype(jnp.float32)
                ext[p, 16 : 16 + tokens, :] = proj[p, :, at].astype(jnp.float32)
            for c in range(chunks):
                features = []
                for p in range(3):
                    total = None
                    for j in range(3):
                        term = taps[p, j : j + 1, at] * ext[p, pl.ds(16 - j + c * chunk, chunk), :]
                        total = term if total is None else total + term
                    features.append(total)
                lanes = slice(c * LANES, (c + 1) * LANES)
                q_buf[b, :, lanes] = features[0]
                x_buf[b, :, lanes] = (features[1] * features[2]).astype(jnp.bfloat16)
            rate_down = down_ref[at, :]
            rate_wide = jnp.concatenate([rate_down] * (chunk // LANES), axis=1)
            left = (chunk - 1.0) - iota((LANES, chunk), 1).astype(jnp.float32)
            e_high, e_low = split(jnp.exp(-rate_wide * left))
            both = jnp.dot(
                jnp.concatenate([e_high, e_low], axis=0), x_buf[b], preferred_element_type=jnp.float32
            )
            shape = (LANES, wide)
            same = lax.div(iota(shape, 0), MODES) == lax.div(lax.rem(iota(shape, 1), LANES), GROUP)
            gained = jnp.where(same, both[:LANES] + both[LANES:], 0.0)
            s_buf[b] = gained
            power = jnp.exp(-rate_down * float(chunk))
            running = gained[:, 0:LANES]
            for c in range(1, chunks):
                running = power * running + gained[:, c * LANES : (c + 1) * LANES]
            packed = running[0:MODES]
            for g in range(1, held):
                packed = packed + running[g * MODES : (g + 1) * MODES]
            end[b] = packed

        @pl.loop(1, count)
        def _(k):
            @pl.when(me + k < count)
            def _():
                end_copy(me, k, me + k).start()

        @pl.loop(0, blocks)
        def _(b):
            y_buf[b] = jnp.zeros((chunk, wide), jnp.float32)
            lane = lax.div(lax.rem(iota((WINDOW, wide), 1), LANES), GROUP)
            for w in range(chunk // WINDOW):
                begin = w * WINDOW
                piece = x_buf[b, begin : begin + WINDOW, :].astype(jnp.float32)
                spread = jnp.concatenate(
                    [jnp.where(lane == g, piece, 0.0).astype(jnp.bfloat16) for g in range(held)], axis=0
                )
                y_buf[b, begin:chunk, :] += jnp.dot(
                    table[b, 0 : chunk - begin, :], spread, preferred_element_type=jnp.float32
                )

        state[...] = jnp.zeros_like(state)

        @pl.loop(0, count - 1)
        def _(source):
            @pl.when(source < me)
            def _():
                end_copy(source, 1, me).wait_recv()

                @pl.loop(0, blocks)
                def _(b):
                    rate_down = down_ref[pl.ds(pl.multiple_of(b * LANES, LANES), LANES), :]
                    shape = (LANES, LANES)
                    same = lax.div(iota(shape, 0), MODES) == lax.div(iota(shape, 1), GROUP)
                    arrived = jnp.where(same, jnp.concatenate([landed[source, b]] * held, axis=0), 0.0)
                    state[b] = jnp.exp(-rate_down * float(tokens)) * state[b] + arrived

        @pl.loop(0, blocks)
        def _(b):
            at = pl.ds(pl.multiple_of(b * LANES, LANES), LANES)
            power = jnp.exp(-down_ref[at, :] * float(chunk))
            states = [state[b]]
            for c in range(chunks - 1):
                states.append(power * states[-1] + s_buf[b, :, c * LANES : (c + 1) * LANES])
            s_high, s_low = split(jnp.concatenate(states, axis=1))
            lag = iota((chunk, LANES), 0).astype(jnp.float32) + 1.0
            d_high, d_low = split(jnp.exp(-row_ref[b, 0:1, :] * lag) * row_ref[b, 1:2, :])
            carried = jnp.dot(
                jnp.concatenate([d_high, d_high, d_low], axis=1),
                jnp.concatenate([s_high, s_low, s_high], axis=0),
                preferred_element_type=jnp.float32,
            )
            mixed = (q_buf[b] * (y_buf[b] + carried)).astype(jnp.bfloat16)
            for c in range(chunks):
                out[c * chunk : (c + 1) * chunk, at] = mixed[:, c * LANES : (c + 1) * LANES]

        @pl.when(me < count - 1)
        def _():
            halo_copy(me + 1).wait_send()

        @pl.loop(1, count)
        def _(k):
            @pl.when(me + k < count)
            def _():
                end_copy(me, k, me + k).wait_send()

    return pl.pallas_call(
        kernel,
        out_shape=jax.ShapeDtypeStruct((tokens, channels), jnp.bfloat16),
        in_specs=[pl.BlockSpec(memory_space=pltpu.VMEM)] * 4,
        out_specs=pl.BlockSpec(memory_space=pltpu.VMEM),
        scratch_shapes=[
            pltpu.VMEM((3, 16, channels), jnp.bfloat16),
            pltpu.VMEM((3, 16 + tokens, LANES), jnp.float32),
            pltpu.VMEM((blocks, chunk, held * WINDOW), jnp.bfloat16),
            pltpu.VMEM((blocks, chunk, wide), jnp.float32),
            pltpu.VMEM((blocks, chunk, wide), jnp.bfloat16),
            pltpu.VMEM((blocks, LANES, wide), jnp.float32),
            pltpu.VMEM((blocks, chunk, wide), jnp.float32),
            pltpu.VMEM((blocks, MODES, LANES), jnp.float32),
            pltpu.VMEM((count, blocks, MODES, LANES), jnp.float32),
            pltpu.VMEM((blocks, LANES, LANES), jnp.float32),
            pltpu.SemaphoreType.DMA,
            pltpu.SemaphoreType.DMA,
            pltpu.SemaphoreType.DMA((count,)),
            pltpu.SemaphoreType.DMA((count,)),
        ],
        compiler_params=pltpu.CompilerParams(
            collective_id=1, has_side_effects=True, vmem_limit_bytes=48 * 1024 * 1024
        ),
    )(projected, short_filter, rows, down)


def tile_count(chips):
    return max(1, 32 // chips)


def project_and_scatter(mixed, out_weight):
    tokens, depth = mixed.shape
    width = out_weight.shape[1]
    ranks = lax.axis_size("tp")
    chips = ranks // 2
    rows = tokens // ranks
    tiles = tile_count(chips)
    cols = width // tiles
    piece = min(256, cols)
    lag = 2
    slots = (chips - 1) * tiles

    def kernel(mixed_ref, w_ref, out_ref, w_buf, acc, stage, sib, inc,
               w_sem, sib_send, sib_recv, fwd_send, in_recv, out_sem):
        rank = lax.axis_index("tp")
        z = lax.div(rank, 2)
        core = lax.rem(rank, 2)
        partner = z * 2 + (1 - core)
        above = rank + 2
        below = rank - 2

        def w_copy(i):
            return pltpu.make_async_copy(
                w_ref.at[:, pl.ds(pl.multiple_of(i * cols, cols), cols)], w_buf.at[i], w_sem.at[i]
            )

        @pl.loop(0, tiles)
        def _(i):
            w_copy(i).start()

        barrier = pltpu.get_barrier_semaphore()
        pl.semaphore_signal(barrier, inc=1, device_id={"tp": partner}, device_id_type=MESH)

        @pl.when(z < chips - 1)
        def _():
            pl.semaphore_signal(barrier, inc=1, device_id={"tp": above}, device_id_type=MESH)

        @pl.when(z > 0)
        def _():
            pl.semaphore_signal(barrier, inc=1, device_id={"tp": below}, device_id_type=MESH)

        middle = jnp.logical_and(z > 0, z < chips - 1)

        @pl.when(middle)
        def _():
            pl.semaphore_wait(barrier, 3)

        @pl.when(jnp.logical_not(middle))
        def _():
            pl.semaphore_wait(barrier, 2)

        def sib_copy(dest, i):
            return pltpu.make_async_remote_copy(
                src_ref=stage.at[dest, i], dst_ref=sib.at[dest, i],
                send_sem=sib_send.at[dest, i], recv_sem=sib_recv.at[dest, i],
                device_id={"tp": partner}, device_id_type=MESH,
            )

        def fwd_copy(dest, i, landing, target):
            return pltpu.make_async_remote_copy(
                src_ref=acc.at[dest, i], dst_ref=inc.at[landing, i],
                send_sem=fwd_send.at[dest, i], recv_sem=in_recv.at[landing, i],
                device_id={"tp": target}, device_id_type=MESH,
            )

        def compute(dest, i):
            base = dest * (2 * rows)
            own = mixed_ref[pl.ds(pl.multiple_of(base + core * rows, rows), rows), :]
            other = mixed_ref[pl.ds(pl.multiple_of(base + (1 - core) * rows, rows), rows), :]
            left = jnp.concatenate([own, other], axis=0)

            @pl.loop(0, cols // piece)
            def _(p):
                at = pl.ds(pl.multiple_of(p * piece, piece), piece)
                product = jnp.dot(left, w_buf[i, :, at], preferred_element_type=jnp.float32)
                acc[dest, i, :, at] = product[:rows].astype(jnp.bfloat16)
                stage[dest, i, :, at] = product[rows:].astype(jnp.bfloat16)

            sib_copy(dest, i).start()

        def add_in(dest, i, landing):
            @pl.loop(0, cols // piece)
            def _(p):
                at = pl.ds(pl.multiple_of(p * piece, piece), piece)
                total = acc[dest, i, :, at].astype(jnp.float32) + inc[landing, i, :, at].astype(jnp.float32)
                acc[dest, i, :, at] = (total + sib[dest, i, :, at].astype(jnp.float32)).astype(jnp.bfloat16)

        def add_sib(dest, i):
            @pl.loop(0, cols // piece)
            def _(p):
                at = pl.ds(pl.multiple_of(p * piece, piece), piece)
                total = acc[dest, i, :, at].astype(jnp.float32) + sib[dest, i, :, at].astype(jnp.float32)
                acc[dest, i, :, at] = total.astype(jnp.bfloat16)

        def up_place(k):
            return chips - 1 - lax.div(k, tiles), lax.rem(k, tiles)

        def down_place(k):
            return lax.div(k, tiles), lax.rem(k, tiles)

        up_count = (chips - 1 - z) * tiles
        down_count = z * tiles
        up_shift = z * lag
        down_shift = (chips - 1 - z) * lag
        up_first = jnp.where(z < chips - 1, up_shift, slots + lag * chips)
        down_first = jnp.where(z > 0, down_shift, slots + lag * chips)
        first = jnp.minimum(up_first, down_first)

        def forward(k, place, fed, landing_of, target):
            dest, i = place(k)

            @pl.when(k >= 2)
            def _():
                before, j = place(k - 2)
                fwd_copy(before, j, landing_of(before), target).wait_send()

            sib_copy(dest, i).wait_recv()

            @pl.when(fed)
            def _():
                fwd_copy(dest, i, dest, target).wait_recv()
                add_in(dest, i, dest)

            @pl.when(jnp.logical_not(fed))
            def _():
                add_sib(dest, i)

            fwd_copy(dest, i, landing_of(dest), target).start()

        def up_landing(dest):
            return dest

        def down_landing(dest):
            return jnp.where(dest == z - 1, chips, dest)

        @pl.loop(0, slots + 1)
        def _(it):
            w_at = it - first

            @pl.when(jnp.logical_and(w_at >= 0, w_at < tiles))
            def _():
                w_copy(w_at).wait()

            ku = it - up_shift

            @pl.when(jnp.logical_and(ku >= 0, ku < up_count))
            def _():
                dest, i = up_place(ku)
                compute(dest, i)

            kd = it - down_shift

            @pl.when(jnp.logical_and(kd >= 0, kd < down_count))
            def _():
                dest, i = down_place(kd)
                compute(dest, i)

            ks = it - first - tiles

            @pl.when(jnp.logical_and(ks >= 0, ks < tiles))
            def _():
                compute(z, ks)

            @pl.when(jnp.logical_and(ku >= 1, ku <= up_count))
            def _():
                forward(ku - 1, up_place, z > 0, up_landing, above)

            @pl.when(jnp.logical_and(kd >= 1, kd <= down_count))
            def _():
                forward(kd - 1, down_place, z < chips - 1, down_landing, below)

        def drain(count, place, landing_of, target):
            @pl.when(count >= 2)
            def _():
                for back in (2, 1):
                    dest, i = place(count - back)
                    fwd_copy(dest, i, landing_of(dest), target).wait_send()

            @pl.when(count == 1)
            def _():
                dest, i = place(count - 1)
                fwd_copy(dest, i, landing_of(dest), target).wait_send()

        def out_copy(i):
            return pltpu.make_async_copy(
                acc.at[z, i], out_ref.at[:, pl.ds(pl.multiple_of(i * cols, cols), cols)], out_sem.at[i]
            )

        @pl.loop(0, tiles)
        def _(i):
            sib_copy(z, i).wait_recv()

            @pl.when(z < chips - 1)
            def _():
                fwd_copy(z, i, chips, above).wait_recv()

            @pl.when(z > 0)
            def _():
                fwd_copy(z, i, z, below).wait_recv()

            @pl.when(z == 0)
            def _():
                add_in(z, i, chips)

            @pl.when(z == chips - 1)
            def _():
                add_in(z, i, z)

            @pl.when(middle)
            def _():
                @pl.loop(0, cols // piece)
                def _(p):
                    at = pl.ds(pl.multiple_of(p * piece, piece), piece)
                    total = acc[z, i, :, at].astype(jnp.float32) + sib[z, i, :, at].astype(jnp.float32)
                    total = total + inc[z, i, :, at].astype(jnp.float32)
                    total = total + inc[chips, i, :, at].astype(jnp.float32)
                    acc[z, i, :, at] = total.astype(jnp.bfloat16)

            out_copy(i).start()

        drain(up_count, up_place, up_landing, above)
        drain(down_count, down_place, down_landing, below)

        @pl.loop(0, tiles)
        def _(i):
            out_copy(i).wait()

            @pl.loop(0, chips)
            def _(dest):
                sib_copy(dest, i).wait_send()

    block = (chips, tiles, rows, cols)
    return pl.pallas_call(
        kernel,
        out_shape=jax.ShapeDtypeStruct((rows, width), jnp.bfloat16),
        in_specs=[pl.BlockSpec(memory_space=pltpu.VMEM), pl.BlockSpec(memory_space=pl.ANY)],
        out_specs=pl.BlockSpec(memory_space=pl.ANY),
        scratch_shapes=[
            pltpu.VMEM((tiles, depth, cols), jnp.bfloat16),
            pltpu.VMEM(block, jnp.bfloat16),
            pltpu.VMEM(block, jnp.bfloat16),
            pltpu.VMEM(block, jnp.bfloat16),
            pltpu.VMEM((chips + 1, tiles, rows, cols), jnp.bfloat16),
            pltpu.SemaphoreType.DMA((tiles,)),
            pltpu.SemaphoreType.DMA((chips, tiles)),
            pltpu.SemaphoreType.DMA((chips, tiles)),
            pltpu.SemaphoreType.DMA((chips, tiles)),
            pltpu.SemaphoreType.DMA((chips + 1, tiles)),
            pltpu.SemaphoreType.DMA((tiles,)),
        ],
        compiler_params=pltpu.CompilerParams(
            collective_id=0, has_side_effects=True, vmem_limit_bytes=60 * 1024 * 1024
        ),
        cost_estimate=pl.CostEstimate(
            flops=2 * tokens * depth * width, bytes_accessed=2 * depth * width, transcendentals=0
        ),
    )(mixed, out_weight)


def local(projected, short_filter, residue, rate, out_weight):
    mixed = mix(projected, short_filter, residue, rate)
    return project_and_scatter(mixed, out_weight)


def solution(mesh):
    placed = (
        P(None, "seq", "tp"),
        P(None, None, "tp"),
        P("tp", None),
        P("tp", None),
        P("tp", None),
    )
    return jax.shard_map(
        local, mesh=mesh, in_specs=placed, out_specs=P(("seq", "tp"), None), check_vma=False
    )
```

```python
import jax
import jax.numpy as jnp
from jax import lax
from jax.experimental import pallas as pl
from jax.experimental.pallas import tpu as pltpu
from jax.sharding import PartitionSpec as P

GROUP = 16
MODES = 16
MESH = pl.DeviceIdType.MESH
WINDOW = 32
LANES = 128


def split(value):
    high = value.astype(jnp.bfloat16)
    return high, (value - high.astype(jnp.float32)).astype(jnp.bfloat16)


def iota(shape, dim):
    return lax.broadcasted_iota(jnp.int32, shape, dim)


def local(projected, short_filter, residue, rate, out_weight):
    tokens, depth = projected.shape[1:]
    width = out_weight.shape[1]
    blocks = depth // LANES
    held = LANES // GROUP
    count = lax.axis_size("seq")
    ranks = lax.axis_size("tp")
    chips = ranks // 2
    rows = tokens // ranks
    chunk = 2 * rows
    tiles = max(1, 32 // chips)
    cols = width // tiles
    piece = min(256, cols)
    lag = 2
    slots = (chips - 1) * tiles
    mode_weight = residue * jnp.sqrt(-jnp.expm1(-2.0 * rate))
    row_form = jnp.stack([rate.reshape(blocks, LANES), mode_weight.reshape(blocks, LANES)], axis=1)
    column_form = jnp.broadcast_to(rate.reshape(depth, 1), (depth, LANES))

    def kernel(proj, taps, row_ref, down_ref, w_ref, out_ref,
               proj_buf, halo, ext, table, q_buf, x_buf, s_buf, y_buf, end, landed, mixed_ref,
               w_buf, acc, stage, sib, inc, carry,
               proj_sem, halo_send, halo_recv, end_send, end_recv,
               w_sem, sib_send, sib_recv, fwd_send, in_recv, out_sem):
        me = lax.axis_index("seq")
        rank = lax.axis_index("tp")
        z = lax.div(rank, 2)
        core = lax.rem(rank, 2)
        partner = z * 2 + (1 - core)
        above = rank + 2
        below = rank - 2

        def proj_copy(b):
            slot = lax.rem(b, 2)
            return pltpu.make_async_copy(
                proj.at[:, :, pl.ds(pl.multiple_of(b * LANES, LANES), LANES)],
                proj_buf.at[slot], proj_sem.at[slot],
            )

        proj_copy(0).start()
        proj_copy(1).start()

        def w_copy(i):
            return pltpu.make_async_copy(
                w_ref.at[:, pl.ds(pl.multiple_of(i * cols, cols), cols)], w_buf.at[i], w_sem.at[i]
            )

        barrier = pltpu.get_barrier_semaphore()

        @pl.loop(1, count)
        def _(k):
            pl.semaphore_signal(
                barrier, inc=1, device_id={"seq": lax.rem(me + k, count)}, device_id_type=MESH
            )

        pl.semaphore_signal(barrier, inc=1, device_id={"tp": partner}, device_id_type=MESH)

        @pl.when(z < chips - 1)
        def _():
            pl.semaphore_signal(barrier, inc=1, device_id={"tp": above}, device_id_type=MESH)

        @pl.when(z > 0)
        def _():
            pl.semaphore_signal(barrier, inc=1, device_id={"tp": below}, device_id_type=MESH)

        middle = jnp.logical_and(z > 0, z < chips - 1)

        @pl.when(middle)
        def _():
            pl.semaphore_wait(barrier, count + 2)

        @pl.when(jnp.logical_not(middle))
        def _():
            pl.semaphore_wait(barrier, count + 1)

        def halo_copy(target):
            return pltpu.make_async_remote_copy(
                src_ref=proj.at[:, pl.ds(tokens - 16, 16), :], dst_ref=halo,
                send_sem=halo_send, recv_sem=halo_recv,
                device_id={"seq": target}, device_id_type=MESH,
            )

        def end_copy(slot, k, target):
            return pltpu.make_async_remote_copy(
                src_ref=end, dst_ref=landed.at[slot],
                send_sem=end_send.at[k], recv_sem=end_recv.at[slot],
                device_id={"seq": target}, device_id_type=MESH,
            )

        @pl.when(me < count - 1)
        def _():
            halo_copy(me + 1).start()

        @pl.loop(0, blocks)
        def _(b):
            rate_row = row_ref[b, 0:1, :]
            weight_row = row_ref[b, 1:2, :]
            lag = iota((chunk, LANES), 0).astype(jnp.float32) - (WINDOW - 1.0)
            p_high, p_low = split(jnp.exp(-rate_row * lag) * weight_row)
            rate_down = down_ref[pl.ds(pl.multiple_of(b * LANES, LANES), LANES), :]
            rate_down = jnp.concatenate([rate_down] * (held * WINDOW // LANES), axis=1)
            shape = (LANES, held * WINDOW)
            place = lax.rem(iota(shape, 1), WINDOW).astype(jnp.float32) - (WINDOW - 1.0)
            same = lax.div(iota(shape, 0), MODES) == lax.div(iota(shape, 1), WINDOW)
            g_high, g_low = split(jnp.where(same, jnp.exp(rate_down * place), 0.0))
            filled = jnp.dot(
                jnp.concatenate([p_high, p_high, p_low], axis=1),
                jnp.concatenate([g_high, g_low, g_high], axis=0),
                preferred_element_type=jnp.float32,
            )
            shape = (chunk, held * WINDOW)
            causal = iota(shape, 0) >= lax.rem(iota(shape, 1), WINDOW)
            table[b] = jnp.where(causal, filled, 0.0).astype(jnp.bfloat16)

        @pl.loop(0, tiles)
        def _(i):
            w_copy(i).start()

        @pl.when(me > 0)
        def _():
            halo_copy(me).wait_recv()

        @pl.when(me == 0)
        def _():
            halo[...] = jnp.zeros_like(halo)

        @pl.loop(0, blocks)
        def _(b):
            at = pl.ds(pl.multiple_of(b * LANES, LANES), LANES)
            slot = lax.rem(b, 2)
            proj_copy(b).wait()
            for p in range(3):
                ext[p, 0:16, :] = halo[p, :, at].astype(jnp.float32)
                ext[p, 16 : 16 + tokens, :] = proj_buf[slot, p].astype(jnp.float32)

            @pl.when(b + 2 < blocks)
            def _():
                proj_copy(b + 2).start()

            rate_down = down_ref[at, :]
            left = (chunk - 1.0) - iota((LANES, chunk), 1).astype(jnp.float32)
            if chunk > LANES:
                rate_wide = jnp.concatenate([rate_down] * (chunk // LANES), axis=1)
            else:
                rate_wide = rate_down[:, :chunk]
            e_high, e_low = split(jnp.exp(-rate_wide * left))
            decay_out = jnp.concatenate([e_high, e_low], axis=0)
            power = jnp.exp(-rate_down * float(chunk))
            shape = (LANES, LANES)
            same = lax.div(iota(shape, 0), MODES) == lax.div(iota(shape, 1), GROUP)
            running = None
            for c in range(chips):
                features = []
                for p in range(3):
                    total = None
                    for j in range(3):
                        term = taps[p, j : j + 1, at] * ext[p, pl.ds(16 - j + c * chunk, chunk), :]
                        total = term if total is None else total + term
                    features.append(total)
                q_buf[b, c] = features[0]
                signal = (features[1] * features[2]).astype(jnp.bfloat16)
                x_buf[b, c] = signal
                both = jnp.dot(decay_out, signal, preferred_element_type=jnp.float32)
                gained = jnp.where(same, both[:LANES] + both[LANES:], 0.0)
                s_buf[b, c] = gained
                running = gained if running is None else power * running + gained
            packed = running[0:MODES]
            for g in range(1, held):
                packed = packed + running[g * MODES : (g + 1) * MODES]
            end[b] = packed

        @pl.loop(1, count)
        def _(k):
            @pl.when(me + k < count)
            def _():
                end_copy(me, k, me + k).start()

        def settle_states():
            @pl.loop(0, count - 1)
            def _(source):
                @pl.when(source < me)
                def _():
                    end_copy(source, 1, me).wait_recv()

            @pl.loop(0, blocks)
            def _(b):
                rate_down = down_ref[pl.ds(pl.multiple_of(b * LANES, LANES), LANES), :]
                shape = (LANES, LANES)
                same = lax.div(iota(shape, 0), MODES) == lax.div(iota(shape, 1), GROUP)
                whole = jnp.exp(-rate_down * float(tokens))
                power = jnp.exp(-rate_down * float(chunk))
                carry[b] = jnp.zeros(shape, jnp.float32)

                @pl.loop(0, count - 1)
                def _(source):
                    @pl.when(source < me)
                    def _():
                        arrived = jnp.where(same, jnp.concatenate([landed[source, b]] * held, axis=0), 0.0)
                        carry[b] = whole * carry[b] + arrived

                running = carry[b]
                for c in range(chips):
                    gained = s_buf[b, c]
                    s_buf[b, c] = running
                    running = power * running + gained

        def finish(dest, at_first):
            @pl.loop(0, blocks)
            def _(b):
                lane = lax.div(iota((WINDOW, LANES), 1), GROUP)
                y_buf[b] = jnp.zeros((chunk, LANES), jnp.float32)
                for w in range(chunk // WINDOW):
                    begin = w * WINDOW
                    part = x_buf[b, dest, begin : begin + WINDOW, :].astype(jnp.float32)
                    spread = jnp.concatenate(
                        [jnp.where(lane == g, part, 0.0).astype(jnp.bfloat16) for g in range(held)], axis=0
                    )
                    y_buf[b, begin:chunk, :] += jnp.dot(
                        table[b, 0 : chunk - begin, :], spread, preferred_element_type=jnp.float32
                    )

            @pl.when(at_first)
            def _():
                settle_states()

            @pl.loop(0, blocks)
            def _(b):
                at = pl.ds(pl.multiple_of(b * LANES, LANES), LANES)
                s_high, s_low = split(s_buf[b, dest])
                since = iota((chunk, LANES), 0).astype(jnp.float32) + 1.0
                d_high, d_low = split(jnp.exp(-row_ref[b, 0:1, :] * since) * row_ref[b, 1:2, :])
                carried = jnp.dot(
                    jnp.concatenate([d_high, d_high, d_low], axis=1),
                    jnp.concatenate([s_high, s_low, s_high], axis=0),
                    preferred_element_type=jnp.float32,
                )
                mixed = (q_buf[b, dest] * (y_buf[b] + carried)).astype(jnp.bfloat16)
                mixed_ref[pl.ds(pl.multiple_of(dest * chunk, chunk), chunk), at] = mixed

        def sib_copy(dest, i, lane=0, turn=0):
            return pltpu.make_async_remote_copy(
                src_ref=stage.at[lane, turn], dst_ref=sib.at[dest, i],
                send_sem=sib_send.at[lane, turn], recv_sem=sib_recv.at[dest, i],
                device_id={"tp": partner}, device_id_type=MESH,
            )

        def fwd_copy(dest, i, landing, target):
            return pltpu.make_async_remote_copy(
                src_ref=acc.at[dest, i], dst_ref=inc.at[landing, i],
                send_sem=fwd_send.at[dest, i], recv_sem=in_recv.at[landing, i],
                device_id={"tp": target}, device_id_type=MESH,
            )

        def compute(dest, i, lane, k):
            turn = lax.rem(k, 2)

            @pl.when(k >= 2)
            def _():
                sib_copy(dest, i, lane, turn).wait_send()

            base = dest * (2 * rows)
            own = mixed_ref[pl.ds(pl.multiple_of(base + core * rows, rows), rows), :]
            other = mixed_ref[pl.ds(pl.multiple_of(base + (1 - core) * rows, rows), rows), :]
            left = jnp.concatenate([own, other], axis=0)

            @pl.loop(0, cols // piece)
            def _(p):
                at = pl.ds(pl.multiple_of(p * piece, piece), piece)
                product = jnp.dot(left, w_buf[i, :, at], preferred_element_type=jnp.float32)
                acc[dest, i, :, at] = product[:rows].astype(jnp.bfloat16)
                stage[lane, turn, :, at] = product[rows:].astype(jnp.bfloat16)

            sib_copy(dest, i, lane, turn).start()

        def add_in(dest, i, landing):
            @pl.loop(0, cols // piece)
            def _(p):
                at = pl.ds(pl.multiple_of(p * piece, piece), piece)
                total = acc[dest, i, :, at].astype(jnp.float32) + inc[landing, i, :, at].astype(jnp.float32)
                acc[dest, i, :, at] = (total + sib[dest, i, :, at].astype(jnp.float32)).astype(jnp.bfloat16)

        def add_sib(dest, i):
            @pl.loop(0, cols // piece)
            def _(p):
                at = pl.ds(pl.multiple_of(p * piece, piece), piece)
                total = acc[dest, i, :, at].astype(jnp.float32) + sib[dest, i, :, at].astype(jnp.float32)
                acc[dest, i, :, at] = total.astype(jnp.bfloat16)

        def up_place(k):
            return chips - 1 - lax.div(k, tiles), lax.rem(k, tiles)

        def down_place(k):
            return lax.div(k, tiles), lax.rem(k, tiles)

        up_count = (chips - 1 - z) * tiles
        down_count = z * tiles
        up_shift = z * lag
        down_shift = (chips - 1 - z) * lag
        up_first = jnp.where(z < chips - 1, up_shift, slots + lag * chips)
        down_first = jnp.where(z > 0, down_shift, slots + lag * chips)
        first = jnp.minimum(up_first, down_first)

        def forward(k, place, fed, landing_of, target):
            dest, i = place(k)

            @pl.when(k >= 2)
            def _():
                before, j = place(k - 2)
                fwd_copy(before, j, landing_of(before), target).wait_send()

            sib_copy(dest, i).wait_recv()

            @pl.when(fed)
            def _():
                fwd_copy(dest, i, dest, target).wait_recv()
                add_in(dest, i, dest)

            @pl.when(jnp.logical_not(fed))
            def _():
                add_sib(dest, i)

            fwd_copy(dest, i, landing_of(dest), target).start()

        def up_landing(dest):
            return dest

        def down_landing(dest):
            return jnp.where(dest == z - 1, chips, dest)

        @pl.loop(0, slots + 1)
        def _(it):
            w_at = it - first

            @pl.when(jnp.logical_and(w_at >= 0, w_at < tiles))
            def _():
                w_copy(w_at).wait()

            @pl.loop(0, chips)
            def _(dest):
                needed = jnp.where(dest > z, up_shift + (chips - 1 - dest) * tiles, down_shift + dest * tiles)
                needed = jnp.where(dest == z, first + tiles, needed)

                @pl.when(it == needed)
                def _():
                    finish(dest, it == first)

            ku = it - up_shift

            @pl.when(jnp.logical_and(ku >= 0, ku < up_count))
            def _():
                dest, i = up_place(ku)
                compute(dest, i, 0, ku)

            kd = it - down_shift

            @pl.when(jnp.logical_and(kd >= 0, kd < down_count))
            def _():
                dest, i = down_place(kd)
                compute(dest, i, 1, kd)

            ks = it - first - tiles

            @pl.when(jnp.logical_and(ks >= 0, ks < tiles))
            def _():
                compute(z, ks, 2, ks)

            @pl.when(jnp.logical_and(ku >= 1, ku <= up_count))
            def _():
                forward(ku - 1, up_place, z > 0, up_landing, above)

            @pl.when(jnp.logical_and(kd >= 1, kd <= down_count))
            def _():
                forward(kd - 1, down_place, z < chips - 1, down_landing, below)

        def drain(count, place, landing_of, target):
            @pl.when(count >= 2)
            def _():
                for back in (2, 1):
                    dest, i = place(count - back)
                    fwd_copy(dest, i, landing_of(dest), target).wait_send()

            @pl.when(count == 1)
            def _():
                dest, i = place(count - 1)
                fwd_copy(dest, i, landing_of(dest), target).wait_send()

        def out_copy(i):
            return pltpu.make_async_copy(
                acc.at[z, i], out_ref.at[:, pl.ds(pl.multiple_of(i * cols, cols), cols)], out_sem.at[i]
            )

        @pl.loop(0, tiles)
        def _(i):
            sib_copy(z, i).wait_recv()

            @pl.when(z < chips - 1)
            def _():
                fwd_copy(z, i, chips, above).wait_recv()

            @pl.when(z > 0)
            def _():
                fwd_copy(z, i, z, below).wait_recv()

            @pl.when(z == 0)
            def _():
                add_in(z, i, chips)

            @pl.when(z == chips - 1)
            def _():
                add_in(z, i, z)

            @pl.when(middle)
            def _():
                @pl.loop(0, cols // piece)
                def _(p):
                    at = pl.ds(pl.multiple_of(p * piece, piece), piece)
                    total = acc[z, i, :, at].astype(jnp.float32) + sib[z, i, :, at].astype(jnp.float32)
                    total = total + inc[z, i, :, at].astype(jnp.float32)
                    total = total + inc[chips, i, :, at].astype(jnp.float32)
                    acc[z, i, :, at] = total.astype(jnp.bfloat16)

            out_copy(i).start()

        drain(up_count, up_place, up_landing, above)
        drain(down_count, down_place, down_landing, below)

        @pl.loop(0, tiles)
        def _(i):
            out_copy(i).wait()

        for turn in range(2):
            sib_copy(z, 0, 2, turn).wait_send()

            @pl.when(up_count > 0)
            def _():
                sib_copy(z, 0, 0, turn).wait_send()

            @pl.when(down_count > 0)
            def _():
                sib_copy(z, 0, 1, turn).wait_send()

        @pl.when(me < count - 1)
        def _():
            halo_copy(me + 1).wait_send()

        @pl.loop(1, count)
        def _(k):
            @pl.when(me + k < count)
            def _():
                end_copy(me, k, me + k).wait_send()

    block = (chips, tiles, rows, cols)
    inside = pl.BlockSpec(memory_space=pltpu.VMEM)
    outside = pl.BlockSpec(memory_space=pl.ANY)
    return pl.pallas_call(
        kernel,
        out_shape=jax.ShapeDtypeStruct((rows, width), jnp.bfloat16),
        in_specs=[outside, inside, inside, inside, outside],
        out_specs=outside,
        scratch_shapes=[
            pltpu.VMEM((2, 3, tokens, LANES), jnp.bfloat16),
            pltpu.VMEM((3, 16, depth), jnp.bfloat16),
            pltpu.VMEM((3, 16 + tokens, LANES), jnp.float32),
            pltpu.VMEM((blocks, chunk, held * WINDOW), jnp.bfloat16),
            pltpu.VMEM((blocks, chips, chunk, LANES), jnp.float32),
            pltpu.VMEM((blocks, chips, chunk, LANES), jnp.bfloat16),
            pltpu.VMEM((blocks, chips, LANES, LANES), jnp.float32),
            pltpu.VMEM((blocks, chunk, LANES), jnp.float32),
            pltpu.VMEM((blocks, MODES, LANES), jnp.float32),
            pltpu.VMEM((count, blocks, MODES, LANES), jnp.float32),
            pltpu.VMEM((tokens, depth), jnp.bfloat16),
            pltpu.VMEM((tiles, depth, cols), jnp.bfloat16),
            pltpu.VMEM(block, jnp.bfloat16),
            pltpu.VMEM((3, 2, rows, cols), jnp.bfloat16),
            pltpu.VMEM(block, jnp.bfloat16),
            pltpu.VMEM((chips + 1, tiles, rows, cols), jnp.bfloat16),
            pltpu.VMEM((blocks, LANES, LANES), jnp.float32),
            pltpu.SemaphoreType.DMA((2,)),
            pltpu.SemaphoreType.DMA,
            pltpu.SemaphoreType.DMA,
            pltpu.SemaphoreType.DMA((count,)),
            pltpu.SemaphoreType.DMA((count,)),
            pltpu.SemaphoreType.DMA((tiles,)),
            pltpu.SemaphoreType.DMA((3, 2)),
            pltpu.SemaphoreType.DMA((chips, tiles)),
            pltpu.SemaphoreType.DMA((chips, tiles)),
            pltpu.SemaphoreType.DMA((chips + 1, tiles)),
            pltpu.SemaphoreType.DMA((tiles,)),
        ],
        compiler_params=pltpu.CompilerParams(
            collective_id=0, has_side_effects=True, vmem_limit_bytes=63 * 1024 * 1024
        ),
    )(projected, short_filter, row_form, column_form, out_weight)


def solution(mesh):
    placed = (
        P(None, "seq", "tp"),
        P(None, None, "tp"),
        P("tp", None),
        P("tp", None),
        P("tp", None),
    )
    return jax.shard_map(
        local, mesh=mesh, in_specs=placed, out_specs=P(("seq", "tp"), None), check_vma=False
    )
```

```python
import jax
import jax.numpy as jnp
from jax import lax
from jax.experimental import pallas as pl
from jax.experimental.pallas import tpu as pltpu
from jax.sharding import PartitionSpec as P

GROUP = 16
MODES = 16
MESH = pl.DeviceIdType.MESH
WINDOW = 32
LANES = 128


def split(value):
    high = value.astype(jnp.bfloat16)
    return high, (value - high.astype(jnp.float32)).astype(jnp.bfloat16)


def iota(shape, dim):
    return lax.broadcasted_iota(jnp.int32, shape, dim)


def local(projected, short_filter, residue, rate, out_weight):
    tokens, depth = projected.shape[1:]
    width = out_weight.shape[1]
    blocks = depth // LANES
    held = LANES // GROUP
    count = lax.axis_size("seq")
    ranks = lax.axis_size("tp")
    chips = ranks // 2
    rows = tokens // ranks
    chunk = 2 * rows
    tiles = max(1, 32 // chips)
    cols = width // tiles
    piece = min(256, cols)
    lag = 2
    flying = 3
    slots = (chips - 1) * tiles
    mode_weight = residue * jnp.sqrt(-jnp.expm1(-2.0 * rate))

    def kernel(proj, taps, rate_ref, weight_ref, w_ref, out_ref,
               proj_buf, halo, ext, q_ext, down_ref, table, q_buf, x_buf, s_buf, y_buf, end, landed, mixed_ref,
               w_buf, acc, stage, sib, inc, carry,
               proj_sem, halo_send, halo_recv, end_send, end_recv,
               w_sem, sib_send, sib_recv, fwd_send, in_recv, out_sem):
        me = lax.axis_index("seq")
        rank = lax.axis_index("tp")
        z = lax.div(rank, 2)
        core = lax.rem(rank, 2)
        partner = z * 2 + (1 - core)
        above = rank + 2
        below = rank - 2

        def proj_copy(b):
            slot = lax.rem(b, 2)
            return pltpu.make_async_copy(
                proj.at[:, :, pl.ds(pl.multiple_of(b * LANES, LANES), LANES)],
                proj_buf.at[slot], proj_sem.at[slot],
            )

        proj_copy(0).start()
        proj_copy(1).start()

        def w_copy(i):
            return pltpu.make_async_copy(
                w_ref.at[:, pl.ds(pl.multiple_of(i * cols, cols), cols)], w_buf.at[i], w_sem.at[i]
            )

        barrier = pltpu.get_barrier_semaphore()

        @pl.loop(1, count)
        def _(k):
            pl.semaphore_signal(
                barrier, inc=1, device_id={"seq": lax.rem(me + k, count)}, device_id_type=MESH
            )

        pl.semaphore_signal(barrier, inc=1, device_id={"tp": partner}, device_id_type=MESH)

        @pl.when(z < chips - 1)
        def _():
            pl.semaphore_signal(barrier, inc=1, device_id={"tp": above}, device_id_type=MESH)

        @pl.when(z > 0)
        def _():
            pl.semaphore_signal(barrier, inc=1, device_id={"tp": below}, device_id_type=MESH)

        middle = jnp.logical_and(z > 0, z < chips - 1)

        @pl.when(middle)
        def _():
            pl.semaphore_wait(barrier, count + 2)

        @pl.when(jnp.logical_not(middle))
        def _():
            pl.semaphore_wait(barrier, count + 1)

        def halo_copy(target):
            return pltpu.make_async_remote_copy(
                src_ref=proj.at[:, pl.ds(tokens - 16, 16), :], dst_ref=halo,
                send_sem=halo_send, recv_sem=halo_recv,
                device_id={"seq": target}, device_id_type=MESH,
            )

        def end_copy(slot, k, target):
            return pltpu.make_async_remote_copy(
                src_ref=end, dst_ref=landed.at[slot],
                send_sem=end_send.at[k], recv_sem=end_recv.at[slot],
                device_id={"seq": target}, device_id_type=MESH,
            )

        @pl.when(me < count - 1)
        def _():
            halo_copy(me + 1).start()

        @pl.loop(0, blocks)
        def _(b):
            rate_row = rate_ref[pl.ds(b, 1), :]
            weight_row = weight_ref[pl.ds(b, 1), :]
            down_ref[b] = jnp.broadcast_to(rate_row, (LANES, LANES)).T
            lag = iota((chunk, LANES), 0).astype(jnp.float32) - (WINDOW - 1.0)
            p_high, p_low = split(jnp.exp(-rate_row * lag) * weight_row)
            rate_down = jnp.concatenate([down_ref[b]] * (held * WINDOW // LANES), axis=1)
            shape = (LANES, held * WINDOW)
            place = lax.rem(iota(shape, 1), WINDOW).astype(jnp.float32) - (WINDOW - 1.0)
            same = lax.div(iota(shape, 0), MODES) == lax.div(iota(shape, 1), WINDOW)
            g_high, g_low = split(jnp.where(same, jnp.exp(rate_down * place), 0.0))
            filled = jnp.dot(
                jnp.concatenate([p_high, p_high, p_low], axis=1),
                jnp.concatenate([g_high, g_low, g_high], axis=0),
                preferred_element_type=jnp.float32,
            )
            shape = (chunk, held * WINDOW)
            causal = iota(shape, 0) >= lax.rem(iota(shape, 1), WINDOW)
            table[b] = jnp.where(causal, filled, 0.0).astype(jnp.bfloat16)

        @pl.loop(0, tiles)
        def _(i):
            w_copy(i).start()

        @pl.when(me > 0)
        def _():
            halo_copy(me).wait_recv()

        @pl.when(me == 0)
        def _():
            halo[...] = jnp.zeros_like(halo)

        @pl.loop(0, blocks)
        def _(b):
            at = pl.ds(pl.multiple_of(b * LANES, LANES), LANES)
            slot = lax.rem(b, 2)
            proj_copy(b).wait()
            q_buf[b, 0:16, :] = halo[0, :, at]
            q_buf[b, 16 : 16 + tokens, :] = proj_buf[slot, 0]
            for p in (1, 2):
                ext[p - 1, 0:16, :] = halo[p, :, at].astype(jnp.float32)
                ext[p - 1, 16 : 16 + tokens, :] = proj_buf[slot, p].astype(jnp.float32)

            @pl.when(b + 2 < blocks)
            def _():
                proj_copy(b + 2).start()

            rate_down = down_ref[b]
            left = (chunk - 1.0) - iota((LANES, chunk), 1).astype(jnp.float32)
            if chunk > LANES:
                rate_wide = jnp.concatenate([rate_down] * (chunk // LANES), axis=1)
            else:
                rate_wide = rate_down[:, :chunk]
            e_high, e_low = split(jnp.exp(-rate_wide * left))
            decay_out = jnp.concatenate([e_high, e_low], axis=0)
            power = jnp.exp(-rate_down * float(chunk))
            shape = (LANES, LANES)
            same = lax.div(iota(shape, 0), MODES) == lax.div(iota(shape, 1), GROUP)
            running = None
            for c in range(chips):
                features = []
                for p in (1, 2):
                    total = None
                    for j in range(3):
                        term = taps[p, j : j + 1, at] * ext[p - 1, pl.ds(16 - j + c * chunk, chunk), :]
                        total = term if total is None else total + term
                    features.append(total)
                signal = (features[0] * features[1]).astype(jnp.bfloat16)
                x_buf[b, c] = signal
                both = jnp.dot(decay_out, signal, preferred_element_type=jnp.float32)
                gained = jnp.where(same, both[:LANES] + both[LANES:], 0.0)
                s_buf[b, c] = gained
                running = gained if running is None else power * running + gained
            packed = running[0:MODES]
            for g in range(1, held):
                packed = packed + running[g * MODES : (g + 1) * MODES]
            end[b] = packed

        @pl.loop(1, count)
        def _(k):
            @pl.when(me + k < count)
            def _():
                end_copy(me, k, me + k).start()

        def settle_states():
            @pl.loop(0, count - 1)
            def _(source):
                @pl.when(source < me)
                def _():
                    end_copy(source, 1, me).wait_recv()

            @pl.loop(0, blocks)
            def _(b):
                rate_down = down_ref[b]
                shape = (LANES, LANES)
                same = lax.div(iota(shape, 0), MODES) == lax.div(iota(shape, 1), GROUP)
                whole = jnp.exp(-rate_down * float(tokens))
                power = jnp.exp(-rate_down * float(chunk))
                carry[b] = jnp.zeros(shape, jnp.float32)

                @pl.loop(0, count - 1)
                def _(source):
                    @pl.when(source < me)
                    def _():
                        arrived = jnp.where(same, jnp.concatenate([landed[source, b]] * held, axis=0), 0.0)
                        carry[b] = whole * carry[b] + arrived

                running = carry[b]
                for c in range(chips):
                    gained = s_buf[b, c]
                    s_buf[b, c] = running
                    running = power * running + gained

        def convolve(dest, b):
            lane = lax.div(iota((WINDOW, LANES), 1), GROUP)
            y_buf[b] = jnp.zeros((chunk, LANES), jnp.float32)
            for w in range(chunk // WINDOW):
                begin = w * WINDOW
                part = x_buf[b, dest, begin : begin + WINDOW, :].astype(jnp.float32)
                spread = jnp.concatenate(
                    [jnp.where(lane == g, part, 0.0).astype(jnp.bfloat16) for g in range(held)], axis=0
                )
                y_buf[b, begin:chunk, :] += jnp.dot(
                    table[b, 0 : chunk - begin, :], spread, preferred_element_type=jnp.float32
                )

        def combine(dest, b):
            at = pl.ds(pl.multiple_of(b * LANES, LANES), LANES)
            start = pl.multiple_of(dest * chunk, chunk)
            q_ext[...] = q_buf[b, pl.ds(start, chunk + 16), :].astype(jnp.float32)
            query = None
            for j in range(3):
                term = taps[0, j : j + 1, at] * q_ext[16 - j : 16 - j + chunk, :]
                query = term if query is None else query + term
            s_high, s_low = split(s_buf[b, dest])
            since = iota((chunk, LANES), 0).astype(jnp.float32) + 1.0
            d_high, d_low = split(jnp.exp(-rate_ref[pl.ds(b, 1), :] * since) * weight_ref[pl.ds(b, 1), :])
            carried = jnp.dot(
                jnp.concatenate([d_high, d_high, d_low], axis=1),
                jnp.concatenate([s_high, s_low, s_high], axis=0),
                preferred_element_type=jnp.float32,
            )
            mixed_ref[pl.ds(start, chunk), at] = (query * (y_buf[b] + carried)).astype(jnp.bfloat16)

        def sib_copy(dest, i, lane=0, turn=0):
            return pltpu.make_async_remote_copy(
                src_ref=stage.at[lane, turn], dst_ref=sib.at[dest, i],
                send_sem=sib_send.at[lane, turn], recv_sem=sib_recv.at[dest, i],
                device_id={"tp": partner}, device_id_type=MESH,
            )

        def fwd_copy(dest, i, landing, target):
            return pltpu.make_async_remote_copy(
                src_ref=acc.at[dest, i], dst_ref=inc.at[landing, i],
                send_sem=fwd_send.at[dest, i], recv_sem=in_recv.at[landing, i],
                device_id={"tp": target}, device_id_type=MESH,
            )

        def compute(dest, i, lane, k):
            turn = lax.rem(k, 2)

            @pl.when(k >= 2)
            def _():
                sib_copy(dest, i, lane, turn).wait_send()

            base = dest * (2 * rows)
            own = mixed_ref[pl.ds(pl.multiple_of(base + core * rows, rows), rows), :]
            other = mixed_ref[pl.ds(pl.multiple_of(base + (1 - core) * rows, rows), rows), :]
            left = jnp.concatenate([own, other], axis=0)

            @pl.loop(0, cols // piece)
            def _(p):
                at = pl.ds(pl.multiple_of(p * piece, piece), piece)
                product = jnp.dot(left, w_buf[i, :, at], preferred_element_type=jnp.float32)
                acc[dest, i, :, at] = product[:rows].astype(jnp.bfloat16)
                stage[lane, turn, :, at] = product[rows:].astype(jnp.bfloat16)

            sib_copy(dest, i, lane, turn).start()

        def add_in(dest, i, landing):
            @pl.loop(0, cols // piece)
            def _(p):
                at = pl.ds(pl.multiple_of(p * piece, piece), piece)
                total = acc[dest, i, :, at].astype(jnp.float32) + inc[landing, i, :, at].astype(jnp.float32)
                acc[dest, i, :, at] = (total + sib[dest, i, :, at].astype(jnp.float32)).astype(jnp.bfloat16)

        def add_sib(dest, i):
            @pl.loop(0, cols // piece)
            def _(p):
                at = pl.ds(pl.multiple_of(p * piece, piece), piece)
                total = acc[dest, i, :, at].astype(jnp.float32) + sib[dest, i, :, at].astype(jnp.float32)
                acc[dest, i, :, at] = total.astype(jnp.bfloat16)

        def up_place(k):
            return chips - 1 - lax.div(k, tiles), lax.rem(k, tiles)

        def down_place(k):
            return lax.div(k, tiles), lax.rem(k, tiles)

        up_count = (chips - 1 - z) * tiles
        down_count = z * tiles
        up_shift = z * lag
        down_shift = (chips - 1 - z) * lag
        up_first = jnp.where(z < chips - 1, up_shift, slots + lag * chips)
        down_first = jnp.where(z > 0, down_shift, slots + lag * chips)
        first = jnp.minimum(up_first, down_first)
        self_first = first + tiles + tiles // 2
        share = -(-blocks // tiles)

        def forward(k, place, fed, landing_of, target):
            dest, i = place(k)

            @pl.when(k >= flying)
            def _():
                before, j = place(k - flying)
                fwd_copy(before, j, landing_of(before), target).wait_send()

            sib_copy(dest, i).wait_recv()

            @pl.when(fed)
            def _():
                fwd_copy(dest, i, dest, target).wait_recv()
                add_in(dest, i, dest)

            @pl.when(jnp.logical_not(fed))
            def _():
                add_sib(dest, i)

            fwd_copy(dest, i, landing_of(dest), target).start()

        def up_landing(dest):
            return dest

        def down_landing(dest):
            return jnp.where(dest == z - 1, chips, dest)

        @pl.loop(0, slots + 1)
        def _(it):
            w_at = it - first

            @pl.when(jnp.logical_and(w_at >= 0, w_at < tiles))
            def _():
                w_copy(w_at).wait()

            @pl.when(it == first)
            def _():
                dest = jnp.where(first == up_first, chips - 1, 0)

                @pl.loop(0, blocks)
                def _(b):
                    convolve(dest, b)

                settle_states()

                @pl.loop(0, blocks)
                def _(b):
                    combine(dest, b)

            @pl.loop(0, chips)
            def _(dest):
                needed = jnp.where(dest > z, up_shift + (chips - 1 - dest) * tiles, down_shift + dest * tiles)
                needed = jnp.where(dest == z, self_first, needed)
                turn = it - needed + tiles - 1
                gradual = needed - tiles + 1 > first
                inside = jnp.logical_and(turn >= 0, turn < tiles)
                low = jnp.where(gradual, turn * share, 0)
                high = jnp.where(gradual, jnp.minimum(low + share, blocks), blocks)
                active = jnp.logical_and(needed != first, jnp.where(gradual, inside, it == needed))
                high = jnp.where(active, high, low)

                @pl.loop(low, high)
                def _(b):
                    convolve(dest, b)
                    combine(dest, b)

            ku = it - up_shift

            @pl.when(jnp.logical_and(ku >= 0, ku < up_count))
            def _():
                dest, i = up_place(ku)
                compute(dest, i, 0, ku)

            kd = it - down_shift

            @pl.when(jnp.logical_and(kd >= 0, kd < down_count))
            def _():
                dest, i = down_place(kd)
                compute(dest, i, 1, kd)

            ks = it - self_first

            @pl.when(jnp.logical_and(ks >= 0, ks < tiles))
            def _():
                compute(z, ks, 2, ks)

            @pl.when(jnp.logical_and(ku >= 1, ku <= up_count))
            def _():
                forward(ku - 1, up_place, z > 0, up_landing, above)

            @pl.when(jnp.logical_and(kd >= 1, kd <= down_count))
            def _():
                forward(kd - 1, down_place, z < chips - 1, down_landing, below)

        def drain(count, place, landing_of, target):
            for back in range(flying, 0, -1):
                @pl.when(count >= back)
                def _():
                    dest, i = place(count - back)
                    fwd_copy(dest, i, landing_of(dest), target).wait_send()

        def out_copy(i):
            return pltpu.make_async_copy(
                acc.at[z, i], out_ref.at[:, pl.ds(pl.multiple_of(i * cols, cols), cols)], out_sem.at[i]
            )

        @pl.loop(0, tiles)
        def _(i):
            sib_copy(z, i).wait_recv()

            @pl.when(z < chips - 1)
            def _():
                fwd_copy(z, i, chips, above).wait_recv()

            @pl.when(z > 0)
            def _():
                fwd_copy(z, i, z, below).wait_recv()

            @pl.when(z == 0)
            def _():
                add_in(z, i, chips)

            @pl.when(z == chips - 1)
            def _():
                add_in(z, i, z)

            @pl.when(middle)
            def _():
                @pl.loop(0, cols // piece)
                def _(p):
                    at = pl.ds(pl.multiple_of(p * piece, piece), piece)
                    total = acc[z, i, :, at].astype(jnp.float32) + sib[z, i, :, at].astype(jnp.float32)
                    total = total + inc[z, i, :, at].astype(jnp.float32)
                    total = total + inc[chips, i, :, at].astype(jnp.float32)
                    acc[z, i, :, at] = total.astype(jnp.bfloat16)

            out_copy(i).start()

        drain(up_count, up_place, up_landing, above)
        drain(down_count, down_place, down_landing, below)

        @pl.loop(0, tiles)
        def _(i):
            out_copy(i).wait()

        for turn in range(2):
            sib_copy(z, 0, 2, turn).wait_send()

            @pl.when(up_count > 0)
            def _():
                sib_copy(z, 0, 0, turn).wait_send()

            @pl.when(down_count > 0)
            def _():
                sib_copy(z, 0, 1, turn).wait_send()

        @pl.when(me < count - 1)
        def _():
            halo_copy(me + 1).wait_send()

        @pl.loop(1, count)
        def _(k):
            @pl.when(me + k < count)
            def _():
                end_copy(me, k, me + k).wait_send()

    block = (chips, tiles, rows, cols)
    inside = pl.BlockSpec(memory_space=pltpu.VMEM)
    outside = pl.BlockSpec(memory_space=pl.ANY)
    return pl.pallas_call(
        kernel,
        out_shape=jax.ShapeDtypeStruct((rows, width), jnp.bfloat16),
        in_specs=[outside, inside, inside, inside, outside],
        out_specs=outside,
        scratch_shapes=[
            pltpu.VMEM((2, 3, tokens, LANES), jnp.bfloat16),
            pltpu.VMEM((3, 16, depth), jnp.bfloat16),
            pltpu.VMEM((2, 16 + tokens, LANES), jnp.float32),
            pltpu.VMEM((16 + chunk, LANES), jnp.float32),
            pltpu.VMEM((blocks, LANES, LANES), jnp.float32),
            pltpu.VMEM((blocks, chunk, held * WINDOW), jnp.bfloat16),
            pltpu.VMEM((blocks, 16 + tokens, LANES), jnp.bfloat16),
            pltpu.VMEM((blocks, chips, chunk, LANES), jnp.bfloat16),
            pltpu.VMEM((blocks, chips, LANES, LANES), jnp.float32),
            pltpu.VMEM((blocks, chunk, LANES), jnp.float32),
            pltpu.VMEM((blocks, MODES, LANES), jnp.float32),
            pltpu.VMEM((count, blocks, MODES, LANES), jnp.float32),
            pltpu.VMEM((tokens, depth), jnp.bfloat16),
            pltpu.VMEM((tiles, depth, cols), jnp.bfloat16),
            pltpu.VMEM(block, jnp.bfloat16),
            pltpu.VMEM((3, 2, rows, cols), jnp.bfloat16),
            pltpu.VMEM(block, jnp.bfloat16),
            pltpu.VMEM((chips + 1, tiles, rows, cols), jnp.bfloat16),
            pltpu.VMEM((blocks, LANES, LANES), jnp.float32),
            pltpu.SemaphoreType.DMA((2,)),
            pltpu.SemaphoreType.DMA,
            pltpu.SemaphoreType.DMA,
            pltpu.SemaphoreType.DMA((count,)),
            pltpu.SemaphoreType.DMA((count,)),
            pltpu.SemaphoreType.DMA((tiles,)),
            pltpu.SemaphoreType.DMA((3, 2)),
            pltpu.SemaphoreType.DMA((chips, tiles)),
            pltpu.SemaphoreType.DMA((chips, tiles)),
            pltpu.SemaphoreType.DMA((chips + 1, tiles)),
            pltpu.SemaphoreType.DMA((tiles,)),
        ],
        compiler_params=pltpu.CompilerParams(
            collective_id=0, has_side_effects=True, vmem_limit_bytes=63 * 1024 * 1024
        ),
    )(
        projected, short_filter, rate.reshape(blocks, LANES), mode_weight.reshape(blocks, LANES), out_weight
    )


def solution(mesh):
    placed = (
        P(None, "seq", "tp"),
        P(None, None, "tp"),
        P("tp", None),
        P("tp", None),
        P("tp", None),
    )
    return jax.shard_map(
        local, mesh=mesh, in_specs=placed, out_specs=P(("seq", "tp"), None), check_vma=False
    )
```

```python
import jax
import jax.numpy as jnp
from jax import lax
from jax.experimental import pallas as pl
from jax.experimental.pallas import tpu as pltpu
from jax.sharding import PartitionSpec as P

GROUP = 16
MODES = 16
MESH = pl.DeviceIdType.MESH
WINDOW = 32
LANES = 128


def split(value):
    high = value.astype(jnp.bfloat16)
    return high, (value - high.astype(jnp.float32)).astype(jnp.bfloat16)


def iota(shape, dim):
    return lax.broadcasted_iota(jnp.int32, shape, dim)


def group_of(shape, dim, size):
    return lax.shift_right_logical(iota(shape, dim), size.bit_length() - 1)


def local(projected, short_filter, residue, rate, out_weight):
    tokens, depth = projected.shape[1:]
    width = out_weight.shape[1]
    blocks = depth // LANES
    held = LANES // GROUP
    count = lax.axis_size("seq")
    ranks = lax.axis_size("tp")
    chips = ranks // 2
    rows = tokens // ranks
    chunk = 2 * rows
    tiles = max(1, 32 // chips)
    cols = width // tiles
    piece = min(256, cols)
    lag = 2
    flying = 3
    slots = (chips - 1) * tiles
    mode_weight = residue * jnp.sqrt(-jnp.expm1(-2.0 * rate))

    def kernel(proj, taps, rate_ref, weight_ref, w_ref, out_ref,
               proj_buf, halo, ext, q_ext, down_ref, table, q_buf, x_buf, s_buf, y_buf, end, landed, mixed_ref,
               w_buf, acc, stage, sib, inc, carry,
               proj_sem, halo_send, halo_recv, end_send, end_recv,
               w_sem, sib_send, sib_recv, fwd_send, in_recv, out_sem):
        me = lax.axis_index("seq")
        rank = lax.axis_index("tp")
        z = lax.div(rank, 2)
        core = lax.rem(rank, 2)
        partner = z * 2 + (1 - core)
        above = rank + 2
        below = rank - 2

        def proj_copy(b):
            slot = lax.rem(b, 2)
            return pltpu.make_async_copy(
                proj.at[:, :, pl.ds(pl.multiple_of(b * LANES, LANES), LANES)],
                proj_buf.at[slot], proj_sem.at[slot],
            )

        proj_copy(0).start()
        proj_copy(1).start()

        def w_copy(i):
            return pltpu.make_async_copy(
                w_ref.at[:, pl.ds(pl.multiple_of(i * cols, cols), cols)], w_buf.at[i], w_sem.at[i]
            )

        barrier = pltpu.get_barrier_semaphore()

        @pl.loop(1, count)
        def _(k):
            pl.semaphore_signal(
                barrier, inc=1, device_id={"seq": lax.rem(me + k, count)}, device_id_type=MESH
            )

        pl.semaphore_signal(barrier, inc=1, device_id={"tp": partner}, device_id_type=MESH)

        @pl.when(z < chips - 1)
        def _():
            pl.semaphore_signal(barrier, inc=1, device_id={"tp": above}, device_id_type=MESH)

        @pl.when(z > 0)
        def _():
            pl.semaphore_signal(barrier, inc=1, device_id={"tp": below}, device_id_type=MESH)

        middle = jnp.logical_and(z > 0, z < chips - 1)

        @pl.when(middle)
        def _():
            pl.semaphore_wait(barrier, count + 2)

        @pl.when(jnp.logical_not(middle))
        def _():
            pl.semaphore_wait(barrier, count + 1)

        def halo_copy(target):
            return pltpu.make_async_remote_copy(
                src_ref=proj.at[:, pl.ds(tokens - 16, 16), :], dst_ref=halo,
                send_sem=halo_send, recv_sem=halo_recv,
                device_id={"seq": target}, device_id_type=MESH,
            )

        def end_copy(slot, k, target):
            return pltpu.make_async_remote_copy(
                src_ref=end, dst_ref=landed.at[slot],
                send_sem=end_send.at[k], recv_sem=end_recv.at[slot],
                device_id={"seq": target}, device_id_type=MESH,
            )

        @pl.when(me < count - 1)
        def _():
            halo_copy(me + 1).start()

        @pl.loop(0, blocks, unroll=2)
        def _(b):
            rate_row = rate_ref[pl.ds(b, 1), :]
            weight_row = weight_ref[pl.ds(b, 1), :]
            down_ref[b] = jnp.broadcast_to(rate_row, (LANES, LANES)).T
            lag = iota((chunk, LANES), 0).astype(jnp.float32) - (WINDOW - 1.0)
            p_high, p_low = split(jnp.exp(-rate_row * lag) * weight_row)
            rate_down = jnp.concatenate([down_ref[b]] * (held * WINDOW // LANES), axis=1)
            shape = (LANES, held * WINDOW)
            place = (iota(shape, 1) & (WINDOW - 1)).astype(jnp.float32) - (WINDOW - 1.0)
            same = group_of(shape, 0, MODES) == group_of(shape, 1, WINDOW)
            g_high, g_low = split(jnp.where(same, jnp.exp(rate_down * place), 0.0))
            filled = jnp.dot(
                jnp.concatenate([p_high, p_high, p_low], axis=1),
                jnp.concatenate([g_high, g_low, g_high], axis=0),
                preferred_element_type=jnp.float32,
            )
            shape = (chunk, held * WINDOW)
            causal = iota(shape, 0) >= (iota(shape, 1) & (WINDOW - 1))
            table[b, 0:chunk, :] = jnp.zeros(shape, jnp.bfloat16)
            table[b, chunk : 2 * chunk, :] = jnp.where(causal, filled, 0.0).astype(jnp.bfloat16)

        @pl.loop(0, tiles)
        def _(i):
            w_copy(i).start()

        @pl.when(me > 0)
        def _():
            halo_copy(me).wait_recv()

        @pl.when(me == 0)
        def _():
            halo[...] = jnp.zeros_like(halo)

        @pl.loop(0, blocks)
        def _(b):
            at = pl.ds(pl.multiple_of(b * LANES, LANES), LANES)
            slot = lax.rem(b, 2)
            proj_copy(b).wait()
            q_buf[b, 0:16, :] = halo[0, :, at]
            q_buf[b, 16 : 16 + tokens, :] = proj_buf[slot, 0]
            for p in (1, 2):
                ext[p - 1, 0:16, :] = halo[p, :, at].astype(jnp.float32)
                ext[p - 1, 16 : 16 + tokens, :] = proj_buf[slot, p].astype(jnp.float32)

            @pl.when(b + 2 < blocks)
            def _():
                proj_copy(b + 2).start()

            rate_down = down_ref[b]
            left = (chunk - 1.0) - iota((LANES, chunk), 1).astype(jnp.float32)
            if chunk > LANES:
                rate_wide = jnp.concatenate([rate_down] * (chunk // LANES), axis=1)
            else:
                rate_wide = rate_down[:, :chunk]
            e_high, e_low = split(jnp.exp(-rate_wide * left))
            decay_out = jnp.concatenate([e_high, e_low], axis=0)
            power = jnp.exp(-rate_down * float(chunk))
            shape = (LANES, LANES)
            same = group_of(shape, 0, MODES) == group_of(shape, 1, GROUP)
            running = None
            for c in range(chips):
                features = []
                for p in (1, 2):
                    total = None
                    for j in range(3):
                        term = taps[p, j : j + 1, at] * ext[p - 1, pl.ds(16 - j + c * chunk, chunk), :]
                        total = term if total is None else total + term
                    features.append(total)
                signal = (features[0] * features[1]).astype(jnp.bfloat16)
                x_buf[b, c] = signal
                both = jnp.dot(decay_out, signal, preferred_element_type=jnp.float32)
                gained = jnp.where(same, both[:LANES] + both[LANES:], 0.0)
                s_buf[b, c] = gained
                running = gained if running is None else power * running + gained
            packed = running[0:MODES]
            for g in range(1, held):
                packed = packed + running[g * MODES : (g + 1) * MODES]
            end[b] = packed

        @pl.loop(1, count)
        def _(k):
            @pl.when(me + k < count)
            def _():
                end_copy(me, k, me + k).start()

        def settle_states():
            @pl.loop(0, count - 1)
            def _(source):
                @pl.when(source < me)
                def _():
                    end_copy(source, 1, me).wait_recv()

            @pl.loop(0, blocks)
            def _(b):
                rate_down = down_ref[b]
                shape = (LANES, LANES)
                same = group_of(shape, 0, MODES) == group_of(shape, 1, GROUP)
                whole = jnp.exp(-rate_down * float(tokens))
                power = jnp.exp(-rate_down * float(chunk))
                carry[b] = jnp.zeros(shape, jnp.float32)

                @pl.loop(0, count - 1)
                def _(source):
                    @pl.when(source < me)
                    def _():
                        arrived = jnp.where(same, jnp.concatenate([landed[source, b]] * held, axis=0), 0.0)
                        carry[b] = whole * carry[b] + arrived

                running = carry[b]
                for c in range(chips):
                    gained = s_buf[b, c]
                    s_buf[b, c] = running
                    running = power * running + gained

        def convolve(dest, b):
            lane = group_of((WINDOW, LANES), 1, GROUP)
            shifted, spread = [], []
            for w in range(chunk // WINDOW):
                begin = w * WINDOW
                part = x_buf[b, dest, begin : begin + WINDOW, :].astype(jnp.float32)
                spread += [jnp.where(lane == g, part, 0.0).astype(jnp.bfloat16) for g in range(held)]
                shifted.append(table[b, chunk - begin : 2 * chunk - begin, :])
            y_buf[b] = jnp.dot(
                jnp.concatenate(shifted, axis=1),
                jnp.concatenate(spread, axis=0),
                preferred_element_type=jnp.float32,
            )

        def combine(dest, b):
            at = pl.ds(pl.multiple_of(b * LANES, LANES), LANES)
            start = pl.multiple_of(dest * chunk, chunk)
            q_ext[...] = q_buf[b, pl.ds(start, chunk + 16), :].astype(jnp.float32)
            query = None
            for j in range(3):
                term = taps[0, j : j + 1, at] * q_ext[16 - j : 16 - j + chunk, :]
                query = term if query is None else query + term
            s_high, s_low = split(s_buf[b, dest])
            since = iota((chunk, LANES), 0).astype(jnp.float32) + 1.0
            d_high, d_low = split(jnp.exp(-rate_ref[pl.ds(b, 1), :] * since) * weight_ref[pl.ds(b, 1), :])
            carried = jnp.dot(
                jnp.concatenate([d_high, d_high, d_low], axis=1),
                jnp.concatenate([s_high, s_low, s_high], axis=0),
                preferred_element_type=jnp.float32,
            )
            mixed_ref[pl.ds(start, chunk), at] = (query * (y_buf[b] + carried)).astype(jnp.bfloat16)

        def sib_copy(dest, i, lane=0, turn=0):
            return pltpu.make_async_remote_copy(
                src_ref=stage.at[lane, turn], dst_ref=sib.at[dest, i],
                send_sem=sib_send.at[lane, turn], recv_sem=sib_recv.at[dest, i],
                device_id={"tp": partner}, device_id_type=MESH,
            )

        def fwd_copy(dest, i, landing, target):
            return pltpu.make_async_remote_copy(
                src_ref=acc.at[dest, i], dst_ref=inc.at[landing, i],
                send_sem=fwd_send.at[dest, i], recv_sem=in_recv.at[landing, i],
                device_id={"tp": target}, device_id_type=MESH,
            )

        def compute(dest, i, lane, k):
            turn = lax.rem(k, 2)

            @pl.when(k >= 2)
            def _():
                sib_copy(dest, i, lane, turn).wait_send()

            base = dest * (2 * rows)
            own = mixed_ref[pl.ds(pl.multiple_of(base + core * rows, rows), rows), :]
            other = mixed_ref[pl.ds(pl.multiple_of(base + (1 - core) * rows, rows), rows), :]
            left = jnp.concatenate([own, other], axis=0)

            @pl.loop(0, cols // piece)
            def _(p):
                at = pl.ds(pl.multiple_of(p * piece, piece), piece)
                product = jnp.dot(left, w_buf[i, :, at], preferred_element_type=jnp.float32)
                acc[dest, i, :, at] = product[:rows].astype(jnp.bfloat16)
                stage[lane, turn, :, at] = product[rows:].astype(jnp.bfloat16)

            sib_copy(dest, i, lane, turn).start()

        def add_in(dest, i, landing):
            @pl.loop(0, cols // piece)
            def _(p):
                at = pl.ds(pl.multiple_of(p * piece, piece), piece)
                total = acc[dest, i, :, at].astype(jnp.float32) + inc[landing, i, :, at].astype(jnp.float32)
                acc[dest, i, :, at] = (total + sib[dest, i, :, at].astype(jnp.float32)).astype(jnp.bfloat16)

        def add_sib(dest, i):
            @pl.loop(0, cols // piece)
            def _(p):
                at = pl.ds(pl.multiple_of(p * piece, piece), piece)
                total = acc[dest, i, :, at].astype(jnp.float32) + sib[dest, i, :, at].astype(jnp.float32)
                acc[dest, i, :, at] = total.astype(jnp.bfloat16)

        def up_place(k):
            return chips - 1 - lax.div(k, tiles), lax.rem(k, tiles)

        def down_place(k):
            return lax.div(k, tiles), lax.rem(k, tiles)

        up_count = (chips - 1 - z) * tiles
        down_count = z * tiles
        up_shift = z * lag
        down_shift = (chips - 1 - z) * lag
        up_first = jnp.where(z < chips - 1, up_shift, slots + lag * chips)
        down_first = jnp.where(z > 0, down_shift, slots + lag * chips)
        first = jnp.minimum(up_first, down_first)
        self_first = first + tiles + tiles // 2
        share = -(-blocks // tiles)

        def forward(k, place, fed, landing_of, target):
            dest, i = place(k)

            @pl.when(k >= flying)
            def _():
                before, j = place(k - flying)
                fwd_copy(before, j, landing_of(before), target).wait_send()

            sib_copy(dest, i).wait_recv()

            @pl.when(fed)
            def _():
                fwd_copy(dest, i, dest, target).wait_recv()
                add_in(dest, i, dest)

            @pl.when(jnp.logical_not(fed))
            def _():
                add_sib(dest, i)

            fwd_copy(dest, i, landing_of(dest), target).start()

        def up_landing(dest):
            return dest

        def down_landing(dest):
            return jnp.where(dest == z - 1, chips, dest)

        @pl.loop(0, slots + 1)
        def _(it):
            w_at = it - first

            @pl.when(jnp.logical_and(w_at >= 0, w_at < tiles))
            def _():
                w_copy(w_at).wait()

            @pl.when(it == first)
            def _():
                dest = jnp.where(first == up_first, chips - 1, 0)

                @pl.loop(0, blocks, unroll=2)
                def _(b):
                    convolve(dest, b)

                settle_states()

                @pl.loop(0, blocks, unroll=2)
                def _(b):
                    combine(dest, b)

            @pl.loop(0, chips)
            def _(dest):
                needed = jnp.where(dest > z, up_shift + (chips - 1 - dest) * tiles, down_shift + dest * tiles)
                needed = jnp.where(dest == z, self_first, needed)
                turn = it - needed + tiles - 1
                gradual = needed - tiles + 1 > first
                inside = jnp.logical_and(turn >= 0, turn < tiles)
                low = jnp.where(gradual, turn * share, 0)
                high = jnp.where(gradual, jnp.minimum(low + share, blocks), blocks)
                active = jnp.logical_and(needed != first, jnp.where(gradual, inside, it == needed))
                high = jnp.where(active, high, low)

                @pl.loop(low, high)
                def _(b):
                    convolve(dest, b)
                    combine(dest, b)

            ku = it - up_shift

            @pl.when(jnp.logical_and(ku >= 0, ku < up_count))
            def _():
                dest, i = up_place(ku)
                compute(dest, i, 0, ku)

            kd = it - down_shift

            @pl.when(jnp.logical_and(kd >= 0, kd < down_count))
            def _():
                dest, i = down_place(kd)
                compute(dest, i, 1, kd)

            ks = it - self_first

            @pl.when(jnp.logical_and(ks >= 0, ks < tiles))
            def _():
                compute(z, ks, 2, ks)

            @pl.when(jnp.logical_and(ku >= 1, ku <= up_count))
            def _():
                forward(ku - 1, up_place, z > 0, up_landing, above)

            @pl.when(jnp.logical_and(kd >= 1, kd <= down_count))
            def _():
                forward(kd - 1, down_place, z < chips - 1, down_landing, below)

        def drain(count, place, landing_of, target):
            for back in range(flying, 0, -1):
                @pl.when(count >= back)
                def _():
                    dest, i = place(count - back)
                    fwd_copy(dest, i, landing_of(dest), target).wait_send()

        def out_copy(i):
            return pltpu.make_async_copy(
                acc.at[z, i], out_ref.at[:, pl.ds(pl.multiple_of(i * cols, cols), cols)], out_sem.at[i]
            )

        @pl.loop(0, tiles)
        def _(i):
            sib_copy(z, i).wait_recv()

            @pl.when(z < chips - 1)
            def _():
                fwd_copy(z, i, chips, above).wait_recv()

            @pl.when(z > 0)
            def _():
                fwd_copy(z, i, z, below).wait_recv()

            @pl.when(z == 0)
            def _():
                add_in(z, i, chips)

            @pl.when(z == chips - 1)
            def _():
                add_in(z, i, z)

            @pl.when(middle)
            def _():
                @pl.loop(0, cols // piece)
                def _(p):
                    at = pl.ds(pl.multiple_of(p * piece, piece), piece)
                    total = acc[z, i, :, at].astype(jnp.float32) + sib[z, i, :, at].astype(jnp.float32)
                    total = total + inc[z, i, :, at].astype(jnp.float32)
                    total = total + inc[chips, i, :, at].astype(jnp.float32)
                    acc[z, i, :, at] = total.astype(jnp.bfloat16)

            out_copy(i).start()

        drain(up_count, up_place, up_landing, above)
        drain(down_count, down_place, down_landing, below)

        @pl.loop(0, tiles)
        def _(i):
            out_copy(i).wait()

        for turn in range(2):
            sib_copy(z, 0, 2, turn).wait_send()

            @pl.when(up_count > 0)
            def _():
                sib_copy(z, 0, 0, turn).wait_send()

            @pl.when(down_count > 0)
            def _():
                sib_copy(z, 0, 1, turn).wait_send()

        @pl.when(me < count - 1)
        def _():
            halo_copy(me + 1).wait_send()

        @pl.loop(1, count)
        def _(k):
            @pl.when(me + k < count)
            def _():
                end_copy(me, k, me + k).wait_send()

    block = (chips, tiles, rows, cols)
    inside = pl.BlockSpec(memory_space=pltpu.VMEM)
    outside = pl.BlockSpec(memory_space=pl.ANY)
    return pl.pallas_call(
        kernel,
        out_shape=jax.ShapeDtypeStruct((rows, width), jnp.bfloat16),
        in_specs=[outside, inside, inside, inside, outside],
        out_specs=outside,
        scratch_shapes=[
            pltpu.VMEM((2, 3, tokens, LANES), jnp.bfloat16),
            pltpu.VMEM((3, 16, depth), jnp.bfloat16),
            pltpu.VMEM((2, 16 + tokens, LANES), jnp.float32),
            pltpu.VMEM((16 + chunk, LANES), jnp.float32),
            pltpu.VMEM((blocks, LANES, LANES), jnp.float32),
            pltpu.VMEM((blocks, 2 * chunk, held * WINDOW), jnp.bfloat16),
            pltpu.VMEM((blocks, 16 + tokens, LANES), jnp.bfloat16),
            pltpu.VMEM((blocks, chips, chunk, LANES), jnp.bfloat16),
            pltpu.VMEM((blocks, chips, LANES, LANES), jnp.float32),
            pltpu.VMEM((blocks, chunk, LANES), jnp.float32),
            pltpu.VMEM((blocks, MODES, LANES), jnp.float32),
            pltpu.VMEM((count, blocks, MODES, LANES), jnp.float32),
            pltpu.VMEM((tokens, depth), jnp.bfloat16),
            pltpu.VMEM((tiles, depth, cols), jnp.bfloat16),
            pltpu.VMEM(block, jnp.bfloat16),
            pltpu.VMEM((3, 2, rows, cols), jnp.bfloat16),
            pltpu.VMEM(block, jnp.bfloat16),
            pltpu.VMEM((chips + 1, tiles, rows, cols), jnp.bfloat16),
            pltpu.VMEM((blocks, LANES, LANES), jnp.float32),
            pltpu.SemaphoreType.DMA((2,)),
            pltpu.SemaphoreType.DMA,
            pltpu.SemaphoreType.DMA,
            pltpu.SemaphoreType.DMA((count,)),
            pltpu.SemaphoreType.DMA((count,)),
            pltpu.SemaphoreType.DMA((tiles,)),
            pltpu.SemaphoreType.DMA((3, 2)),
            pltpu.SemaphoreType.DMA((chips, tiles)),
            pltpu.SemaphoreType.DMA((chips, tiles)),
            pltpu.SemaphoreType.DMA((chips + 1, tiles)),
            pltpu.SemaphoreType.DMA((tiles,)),
        ],
        compiler_params=pltpu.CompilerParams(
            collective_id=0, has_side_effects=True, vmem_limit_bytes=63 * 1024 * 1024
        ),
    )(
        projected, short_filter, rate.reshape(blocks, LANES), mode_weight.reshape(blocks, LANES), out_weight
    )


def solution(mesh):
    placed = (
        P(None, "seq", "tp"),
        P(None, None, "tp"),
        P("tp", None),
        P("tp", None),
        P("tp", None),
    )
    return jax.shard_map(
        local, mesh=mesh, in_specs=placed, out_specs=P(("seq", "tp"), None), check_vma=False
    )
```

```python
import jax
import jax.numpy as jnp
from jax import lax
from jax.experimental import pallas as pl
from jax.experimental.pallas import tpu as pltpu
from jax.sharding import PartitionSpec as P

GROUP = 16
MODES = 16
MESH = pl.DeviceIdType.MESH
WINDOW = 32
LANES = 128


def split(value):
    high = value.astype(jnp.bfloat16)
    return high, (value - high.astype(jnp.float32)).astype(jnp.bfloat16)


def iota(shape, dim):
    return lax.broadcasted_iota(jnp.int32, shape, dim)


def group_of(shape, dim, size):
    return lax.shift_right_logical(iota(shape, dim), size.bit_length() - 1)


def local(projected, short_filter, residue, rate, out_weight):
    tokens, depth = projected.shape[1:]
    width = out_weight.shape[1]
    blocks = depth // LANES
    held = LANES // GROUP
    count = lax.axis_size("seq")
    ranks = lax.axis_size("tp")
    chips = ranks // 2
    rows = tokens // ranks
    chunk = 2 * rows
    tiles = max(1, 32 // chips)
    cols = width // tiles
    piece = min(256, cols)
    lag = 2
    flying = 3
    slots = (chips - 1) * tiles
    mode_weight = residue * jnp.sqrt(-jnp.expm1(-2.0 * rate))

    def kernel(proj, taps, rate_ref, weight_ref, w_ref, out_ref,
               proj_buf, halo, ext, q_ext, down_ref, table, q_buf, x_buf, s_buf, y_buf, end, landed, mixed_ref,
               w_buf, acc, stage, sib, inc, carry,
               proj_sem, query_sem, halo_send, halo_recv, end_send, end_recv,
               w_sem, sib_send, sib_recv, fwd_send, in_recv, out_sem):
        me = lax.axis_index("seq")
        rank = lax.axis_index("tp")
        z = lax.div(rank, 2)
        core = lax.rem(rank, 2)
        partner = z * 2 + (1 - core)
        above = rank + 2
        below = rank - 2

        def proj_copy(b):
            return pltpu.make_async_copy(
                proj.at[pl.ds(1, 2), :, pl.ds(pl.multiple_of(b * LANES, LANES), LANES)],
                proj_buf.at[b], proj_sem.at[b],
            )

        def query_copy(b):
            return pltpu.make_async_copy(
                proj.at[0, :, pl.ds(pl.multiple_of(b * LANES, LANES), LANES)],
                q_buf.at[b, pl.ds(16, tokens), :], query_sem.at[b],
            )

        @pl.loop(0, blocks)
        def _(b):
            proj_copy(b).start()

        def w_copy(i):
            return pltpu.make_async_copy(
                w_ref.at[:, pl.ds(pl.multiple_of(i * cols, cols), cols)], w_buf.at[i], w_sem.at[i]
            )

        barrier = pltpu.get_barrier_semaphore()

        @pl.loop(1, count)
        def _(k):
            pl.semaphore_signal(
                barrier, inc=1, device_id={"seq": lax.rem(me + k, count)}, device_id_type=MESH
            )

        pl.semaphore_signal(barrier, inc=1, device_id={"tp": partner}, device_id_type=MESH)

        @pl.when(z < chips - 1)
        def _():
            pl.semaphore_signal(barrier, inc=1, device_id={"tp": above}, device_id_type=MESH)

        @pl.when(z > 0)
        def _():
            pl.semaphore_signal(barrier, inc=1, device_id={"tp": below}, device_id_type=MESH)

        middle = jnp.logical_and(z > 0, z < chips - 1)

        @pl.when(middle)
        def _():
            pl.semaphore_wait(barrier, count + 2)

        @pl.when(jnp.logical_not(middle))
        def _():
            pl.semaphore_wait(barrier, count + 1)

        def halo_copy(target):
            return pltpu.make_async_remote_copy(
                src_ref=proj.at[:, pl.ds(tokens - 16, 16), :], dst_ref=halo,
                send_sem=halo_send, recv_sem=halo_recv,
                device_id={"seq": target}, device_id_type=MESH,
            )

        def end_copy(slot, k, target):
            return pltpu.make_async_remote_copy(
                src_ref=end, dst_ref=landed.at[slot],
                send_sem=end_send.at[k], recv_sem=end_recv.at[slot],
                device_id={"seq": target}, device_id_type=MESH,
            )

        @pl.when(me < count - 1)
        def _():
            halo_copy(me + 1).start()

        @pl.loop(0, blocks, unroll=2)
        def _(b):
            rate_row = rate_ref[pl.ds(b, 1), :]
            weight_row = weight_ref[pl.ds(b, 1), :]
            down_ref[b] = jnp.broadcast_to(rate_row, (LANES, LANES)).T
            lag = iota((chunk, LANES), 0).astype(jnp.float32) - (WINDOW - 1.0)
            p_high, p_low = split(jnp.exp(-rate_row * lag) * weight_row)
            rate_down = jnp.concatenate([down_ref[b]] * (held * WINDOW // LANES), axis=1)
            shape = (LANES, held * WINDOW)
            place = (iota(shape, 1) & (WINDOW - 1)).astype(jnp.float32) - (WINDOW - 1.0)
            same = group_of(shape, 0, MODES) == group_of(shape, 1, WINDOW)
            g_high, g_low = split(jnp.where(same, jnp.exp(rate_down * place), 0.0))
            filled = jnp.dot(
                jnp.concatenate([p_high, p_high, p_low], axis=1),
                jnp.concatenate([g_high, g_low, g_high], axis=0),
                preferred_element_type=jnp.float32,
            )
            shape = (chunk, held * WINDOW)
            causal = iota(shape, 0) >= (iota(shape, 1) & (WINDOW - 1))
            table[b, 0:chunk, :] = jnp.zeros(shape, jnp.bfloat16)
            table[b, chunk : 2 * chunk, :] = jnp.where(causal, filled, 0.0).astype(jnp.bfloat16)

        @pl.loop(0, blocks)
        def _(b):
            query_copy(b).start()

        @pl.loop(0, tiles)
        def _(i):
            w_copy(i).start()

        @pl.when(me > 0)
        def _():
            halo_copy(me).wait_recv()

        @pl.when(me == 0)
        def _():
            halo[...] = jnp.zeros_like(halo)

        @pl.loop(0, blocks)
        def _(b):
            at = pl.ds(pl.multiple_of(b * LANES, LANES), LANES)
            proj_copy(b).wait()
            q_buf[b, 0:16, :] = halo[0, :, at]
            for p in (1, 2):
                ext[p - 1, 0:16, :] = halo[p, :, at].astype(jnp.float32)
                ext[p - 1, 16 : 16 + tokens, :] = proj_buf[b, p - 1].astype(jnp.float32)

            rate_down = down_ref[b]
            left = (chunk - 1.0) - iota((LANES, chunk), 1).astype(jnp.float32)
            if chunk > LANES:
                rate_wide = jnp.concatenate([rate_down] * (chunk // LANES), axis=1)
            else:
                rate_wide = rate_down[:, :chunk]
            e_high, e_low = split(jnp.exp(-rate_wide * left))
            decay_out = jnp.concatenate([e_high, e_low], axis=0)
            power = jnp.exp(-rate_down * float(chunk))
            shape = (LANES, LANES)
            same = group_of(shape, 0, MODES) == group_of(shape, 1, GROUP)
            running = None
            for c in range(chips):
                features = []
                for p in (1, 2):
                    total = None
                    for j in range(3):
                        term = taps[p, j : j + 1, at] * ext[p - 1, pl.ds(16 - j + c * chunk, chunk), :]
                        total = term if total is None else total + term
                    features.append(total)
                signal = (features[0] * features[1]).astype(jnp.bfloat16)
                x_buf[b, c] = signal
                both = jnp.dot(decay_out, signal, preferred_element_type=jnp.float32)
                gained = jnp.where(same, both[:LANES] + both[LANES:], 0.0)
                s_buf[b, c] = gained
                running = gained if running is None else power * running + gained
            packed = running[0:MODES]
            for g in range(1, held):
                packed = packed + running[g * MODES : (g + 1) * MODES]
            end[b] = packed

        @pl.loop(1, count)
        def _(k):
            @pl.when(me + k < count)
            def _():
                end_copy(me, k, me + k).start()

        @pl.loop(0, blocks)
        def _(b):
            query_copy(b).wait()

        def settle_states():
            @pl.loop(0, count - 1)
            def _(source):
                @pl.when(source < me)
                def _():
                    end_copy(source, 1, me).wait_recv()

            @pl.loop(0, blocks)
            def _(b):
                rate_down = down_ref[b]
                shape = (LANES, LANES)
                same = group_of(shape, 0, MODES) == group_of(shape, 1, GROUP)
                whole = jnp.exp(-rate_down * float(tokens))
                power = jnp.exp(-rate_down * float(chunk))
                carry[b] = jnp.zeros(shape, jnp.float32)

                @pl.loop(0, count - 1)
                def _(source):
                    @pl.when(source < me)
                    def _():
                        arrived = jnp.where(same, jnp.concatenate([landed[source, b]] * held, axis=0), 0.0)
                        carry[b] = whole * carry[b] + arrived

                running = carry[b]
                for c in range(chips):
                    gained = s_buf[b, c]
                    s_buf[b, c] = running
                    running = power * running + gained

        def convolve(dest, b):
            lane = group_of((WINDOW, LANES), 1, GROUP)
            shifted, spread = [], []
            for w in range(chunk // WINDOW):
                begin = w * WINDOW
                part = x_buf[b, dest, begin : begin + WINDOW, :].astype(jnp.float32)
                spread += [jnp.where(lane == g, part, 0.0).astype(jnp.bfloat16) for g in range(held)]
                shifted.append(table[b, chunk - begin : 2 * chunk - begin, :])
            y_buf[b] = jnp.dot(
                jnp.concatenate(shifted, axis=1),
                jnp.concatenate(spread, axis=0),
                preferred_element_type=jnp.float32,
            )

        def combine(dest, b):
            at = pl.ds(pl.multiple_of(b * LANES, LANES), LANES)
            start = pl.multiple_of(dest * chunk, chunk)
            q_ext[...] = q_buf[b, pl.ds(start, chunk + 16), :].astype(jnp.float32)
            query = None
            for j in range(3):
                term = taps[0, j : j + 1, at] * q_ext[16 - j : 16 - j + chunk, :]
                query = term if query is None else query + term
            s_high, s_low = split(s_buf[b, dest])
            since = iota((chunk, LANES), 0).astype(jnp.float32) + 1.0
            d_high, d_low = split(jnp.exp(-rate_ref[pl.ds(b, 1), :] * since) * weight_ref[pl.ds(b, 1), :])
            carried = jnp.dot(
                jnp.concatenate([d_high, d_high, d_low], axis=1),
                jnp.concatenate([s_high, s_low, s_high], axis=0),
                preferred_element_type=jnp.float32,
            )
            mixed_ref[pl.ds(start, chunk), at] = (query * (y_buf[b] + carried)).astype(jnp.bfloat16)

        def sib_copy(dest, i, lane=0, turn=0):
            return pltpu.make_async_remote_copy(
                src_ref=stage.at[lane, turn], dst_ref=sib.at[dest, i],
                send_sem=sib_send.at[lane, turn], recv_sem=sib_recv.at[dest, i],
                device_id={"tp": partner}, device_id_type=MESH,
            )

        def fwd_copy(dest, i, landing, target):
            return pltpu.make_async_remote_copy(
                src_ref=acc.at[dest, i], dst_ref=inc.at[landing, i],
                send_sem=fwd_send.at[dest, i], recv_sem=in_recv.at[landing, i],
                device_id={"tp": target}, device_id_type=MESH,
            )

        def compute(dest, i, lane, k):
            turn = lax.rem(k, 2)

            @pl.when(k >= 2)
            def _():
                sib_copy(dest, i, lane, turn).wait_send()

            base = dest * (2 * rows)
            own = mixed_ref[pl.ds(pl.multiple_of(base + core * rows, rows), rows), :]
            other = mixed_ref[pl.ds(pl.multiple_of(base + (1 - core) * rows, rows), rows), :]
            left = jnp.concatenate([own, other], axis=0)

            @pl.loop(0, cols // piece)
            def _(p):
                at = pl.ds(pl.multiple_of(p * piece, piece), piece)
                product = jnp.dot(left, w_buf[i, :, at], preferred_element_type=jnp.float32)
                acc[dest, i, :, at] = product[:rows].astype(jnp.bfloat16)
                stage[lane, turn, :, at] = product[rows:].astype(jnp.bfloat16)

            sib_copy(dest, i, lane, turn).start()

        def add_in(dest, i, landing):
            @pl.loop(0, cols // piece)
            def _(p):
                at = pl.ds(pl.multiple_of(p * piece, piece), piece)
                total = acc[dest, i, :, at].astype(jnp.float32) + inc[landing, i, :, at].astype(jnp.float32)
                acc[dest, i, :, at] = (total + sib[dest, i, :, at].astype(jnp.float32)).astype(jnp.bfloat16)

        def add_sib(dest, i):
            @pl.loop(0, cols // piece)
            def _(p):
                at = pl.ds(pl.multiple_of(p * piece, piece), piece)
                total = acc[dest, i, :, at].astype(jnp.float32) + sib[dest, i, :, at].astype(jnp.float32)
                acc[dest, i, :, at] = total.astype(jnp.bfloat16)

        def up_place(k):
            return chips - 1 - lax.div(k, tiles), lax.rem(k, tiles)

        def down_place(k):
            return lax.div(k, tiles), lax.rem(k, tiles)

        up_count = (chips - 1 - z) * tiles
        down_count = z * tiles
        up_shift = z * lag
        down_shift = (chips - 1 - z) * lag
        up_first = jnp.where(z < chips - 1, up_shift, slots + lag * chips)
        down_first = jnp.where(z > 0, down_shift, slots + lag * chips)
        first = jnp.minimum(up_first, down_first)
        self_first = first + tiles + tiles // 2
        share = -(-blocks // tiles)

        def forward(k, place, fed, landing_of, target):
            dest, i = place(k)

            @pl.when(k >= flying)
            def _():
                before, j = place(k - flying)
                fwd_copy(before, j, landing_of(before), target).wait_send()

            sib_copy(dest, i).wait_recv()

            @pl.when(fed)
            def _():
                fwd_copy(dest, i, dest, target).wait_recv()
                add_in(dest, i, dest)

            @pl.when(jnp.logical_not(fed))
            def _():
                add_sib(dest, i)

            fwd_copy(dest, i, landing_of(dest), target).start()

        def up_landing(dest):
            return dest

        def down_landing(dest):
            return jnp.where(dest == z - 1, chips, dest)

        @pl.loop(0, slots + 1)
        def _(it):
            w_at = it - first

            @pl.when(jnp.logical_and(w_at >= 0, w_at < tiles))
            def _():
                w_copy(w_at).wait()

            @pl.when(it == first)
            def _():
                dest = jnp.where(first == up_first, chips - 1, 0)

                @pl.loop(0, blocks, unroll=2)
                def _(b):
                    convolve(dest, b)

                settle_states()

                @pl.loop(0, blocks, unroll=2)
                def _(b):
                    combine(dest, b)

            @pl.loop(0, chips)
            def _(dest):
                needed = jnp.where(dest > z, up_shift + (chips - 1 - dest) * tiles, down_shift + dest * tiles)
                needed = jnp.where(dest == z, self_first, needed)
                turn = it - needed + tiles - 1
                gradual = needed - tiles + 1 > first
                inside = jnp.logical_and(turn >= 0, turn < tiles)
                low = jnp.where(gradual, turn * share, 0)
                high = jnp.where(gradual, jnp.minimum(low + share, blocks), blocks)
                active = jnp.logical_and(needed != first, jnp.where(gradual, inside, it == needed))
                high = jnp.where(active, high, low)

                @pl.loop(low, high)
                def _(b):
                    convolve(dest, b)
                    combine(dest, b)

            ku = it - up_shift

            @pl.when(jnp.logical_and(ku >= 0, ku < up_count))
            def _():
                dest, i = up_place(ku)
                compute(dest, i, 0, ku)

            kd = it - down_shift

            @pl.when(jnp.logical_and(kd >= 0, kd < down_count))
            def _():
                dest, i = down_place(kd)
                compute(dest, i, 1, kd)

            ks = it - self_first

            @pl.when(jnp.logical_and(ks >= 0, ks < tiles))
            def _():
                compute(z, ks, 2, ks)

            @pl.when(jnp.logical_and(ku >= 1, ku <= up_count))
            def _():
                forward(ku - 1, up_place, z > 0, up_landing, above)

            @pl.when(jnp.logical_and(kd >= 1, kd <= down_count))
            def _():
                forward(kd - 1, down_place, z < chips - 1, down_landing, below)

        def drain(count, place, landing_of, target):
            for back in range(flying, 0, -1):
                @pl.when(count >= back)
                def _():
                    dest, i = place(count - back)
                    fwd_copy(dest, i, landing_of(dest), target).wait_send()

        def out_copy(i):
            return pltpu.make_async_copy(
                acc.at[z, i], out_ref.at[:, pl.ds(pl.multiple_of(i * cols, cols), cols)], out_sem.at[i]
            )

        @pl.loop(0, tiles)
        def _(i):
            sib_copy(z, i).wait_recv()

            @pl.when(z < chips - 1)
            def _():
                fwd_copy(z, i, chips, above).wait_recv()

            @pl.when(z > 0)
            def _():
                fwd_copy(z, i, z, below).wait_recv()

            @pl.when(z == 0)
            def _():
                add_in(z, i, chips)

            @pl.when(z == chips - 1)
            def _():
                add_in(z, i, z)

            @pl.when(middle)
            def _():
                @pl.loop(0, cols // piece)
                def _(p):
                    at = pl.ds(pl.multiple_of(p * piece, piece), piece)
                    total = acc[z, i, :, at].astype(jnp.float32) + sib[z, i, :, at].astype(jnp.float32)
                    total = total + inc[z, i, :, at].astype(jnp.float32)
                    total = total + inc[chips, i, :, at].astype(jnp.float32)
                    acc[z, i, :, at] = total.astype(jnp.bfloat16)

            out_copy(i).start()

        drain(up_count, up_place, up_landing, above)
        drain(down_count, down_place, down_landing, below)

        @pl.loop(0, tiles)
        def _(i):
            out_copy(i).wait()

        for turn in range(2):
            sib_copy(z, 0, 2, turn).wait_send()

            @pl.when(up_count > 0)
            def _():
                sib_copy(z, 0, 0, turn).wait_send()

            @pl.when(down_count > 0)
            def _():
                sib_copy(z, 0, 1, turn).wait_send()

        @pl.when(me < count - 1)
        def _():
            halo_copy(me + 1).wait_send()

        @pl.loop(1, count)
        def _(k):
            @pl.when(me + k < count)
            def _():
                end_copy(me, k, me + k).wait_send()

    block = (chips, tiles, rows, cols)
    inside = pl.BlockSpec(memory_space=pltpu.VMEM)
    outside = pl.BlockSpec(memory_space=pl.ANY)
    return pl.pallas_call(
        kernel,
        out_shape=jax.ShapeDtypeStruct((rows, width), jnp.bfloat16),
        in_specs=[outside, inside, inside, inside, outside],
        out_specs=outside,
        scratch_shapes=[
            pltpu.VMEM((blocks, 2, tokens, LANES), jnp.bfloat16),
            pltpu.VMEM((3, 16, depth), jnp.bfloat16),
            pltpu.VMEM((2, 16 + tokens, LANES), jnp.float32),
            pltpu.VMEM((16 + chunk, LANES), jnp.float32),
            pltpu.VMEM((blocks, LANES, LANES), jnp.float32),
            pltpu.VMEM((blocks, 2 * chunk, held * WINDOW), jnp.bfloat16),
            pltpu.VMEM((blocks, 16 + tokens, LANES), jnp.bfloat16),
            pltpu.VMEM((blocks, chips, chunk, LANES), jnp.bfloat16),
            pltpu.VMEM((blocks, chips, LANES, LANES), jnp.float32),
            pltpu.VMEM((blocks, chunk, LANES), jnp.float32),
            pltpu.VMEM((blocks, MODES, LANES), jnp.float32),
            pltpu.VMEM((count, blocks, MODES, LANES), jnp.float32),
            pltpu.VMEM((tokens, depth), jnp.bfloat16),
            pltpu.VMEM((tiles, depth, cols), jnp.bfloat16),
            pltpu.VMEM(block, jnp.bfloat16),
            pltpu.VMEM((3, 2, rows, cols), jnp.bfloat16),
            pltpu.VMEM(block, jnp.bfloat16),
            pltpu.VMEM((chips + 1, tiles, rows, cols), jnp.bfloat16),
            pltpu.VMEM((blocks, LANES, LANES), jnp.float32),
            pltpu.SemaphoreType.DMA((blocks,)),
            pltpu.SemaphoreType.DMA((blocks,)),
            pltpu.SemaphoreType.DMA,
            pltpu.SemaphoreType.DMA,
            pltpu.SemaphoreType.DMA((count,)),
            pltpu.SemaphoreType.DMA((count,)),
            pltpu.SemaphoreType.DMA((tiles,)),
            pltpu.SemaphoreType.DMA((3, 2)),
            pltpu.SemaphoreType.DMA((chips, tiles)),
            pltpu.SemaphoreType.DMA((chips, tiles)),
            pltpu.SemaphoreType.DMA((chips + 1, tiles)),
            pltpu.SemaphoreType.DMA((tiles,)),
        ],
        compiler_params=pltpu.CompilerParams(
            collective_id=0, has_side_effects=True, vmem_limit_bytes=63 * 1024 * 1024
        ),
    )(
        projected, short_filter, rate.reshape(blocks, LANES), mode_weight.reshape(blocks, LANES), out_weight
    )


def solution(mesh):
    placed = (
        P(None, "seq", "tp"),
        P(None, None, "tp"),
        P("tp", None),
        P("tp", None),
        P("tp", None),
    )
    return jax.shard_map(
        local, mesh=mesh, in_specs=placed, out_specs=P(("seq", "tp"), None), check_vma=False
    )
```
